32 devices in a mesh: dp: 8 (over y, x, core), expert: 4 (over z).
Axes of the slice: x: 2, y: 2, z: 4, core: 2. Of those that a mesh axis runs over, the one named last changes fastest.
Arguments:
- hidden_in: bfloat16 [4096, 2048], P(('dp', 'expert')), may hold values from -6 to 6
- seq_lengths: int32 [32], P(('dp', 'expert')), may hold values from 32 to 128, as said below
- attn_routes: int32 [4096, 2], P(('dp', 'expert')), may hold values from 0 to 3, all different within a row; in each aligned block of 128 rows (0 to 127, 128 to 255, ...) at most 96 rows name the same one
- attn_gates: float32 [4096, 2], P(('dp', 'expert')), may hold values from 0.25 to 1
- mlp_routes: int32 [4096, 2], P(('dp', 'expert')), may hold values from 0 to 3, all different within a row; in each aligned block of 128 rows (0 to 127, 128 to 255, ...) at most 96 rows name the same one
- mlp_gates: float32 [4096, 2], P(('dp', 'expert')), may hold values from 0.25 to 1
- attn_gain: bfloat16 [2048], P(('dp', 'expert')), may hold values from 0.5 to 1.5
- mlp_gain: bfloat16 [2048], P(('dp', 'expert')), may hold values from 0.5 to 1.5
- k_weight: bfloat16 [2048, 2048], P(('dp', 'expert')), may hold values from -0.125 to 0.125
- v_weight: bfloat16 [2048, 2048], P(('dp', 'expert')), may hold values from -0.125 to 0.125
- attn_experts: bfloat16 [4, 2048, 2, 2048], P('expert', 'dp'), may hold values from -0.25 to 0.25
- mlp_experts: bfloat16 [4, 5632, 3, 2048], P('expert', 'dp'), may hold values from -0.125 to 0.125
- logit_limit: float32 [16], replicated, may hold values from 1.5 to 4.5
- out_grad: bfloat16 [4096, 2048], P(('dp', 'expert')), may hold values from -6 to 6
Outputs:
- block_out: bfloat16 [4096, 2048], P(('dp', 'expert'))
- grad_input: float32 [4096, 2048], P(('dp', 'expert'))
- grad_k_weight: float32 [2048, 2048], P(('dp', 'expert'))
- grad_v_weight: float32 [2048, 2048], P(('dp', 'expert'))
- grad_attn_gain: float32 [2048], P(('dp', 'expert'))
- grad_mlp_gain: float32 [2048], P(('dp', 'expert'))
- grad_attn_experts: float32 [4, 2048, 2, 2048], P('expert', 'dp')
- grad_mlp_experts: float32 [4, 5632, 3, 2048], P('expert', 'dp')
- clipped_query: bfloat16 [4, 2048, 2048], P('expert', 'dp')
- clipped_key: bfloat16 [2048, 2048], P(('dp', 'expert'))
- clip_factors: float32 [16], replicated
The draws below stay inside these ranges and needn't reach their ends.
Inputs may be any that keep to these rules, and one draw needn't show every extreme that they name: `seq_lengths`: one sequence has all 128 slots live in every draw. `attn_routes`: each token names 2 different experts; among the tokens of one sequence no expert is named more than 96 times. `mlp_routes`: each token names 2 different experts; among the tokens of one sequence no expert is named more than 96 times.
All inputs are finite; a program needn't handle non-finite values.
Results may differ from the reference program's by a relative error of at most 0.02.
Values may be sent and summed in bfloat16 or wider, within the bound.
No kernel may reach another device: no remote copies, remote signals or barrier semaphores. Data moves between devices by JAX's collectives and lax.ppermute only.
A program may use at most 704 MiB of HBM per device.

```python
import math
import jax
import jax.numpy as jnp
import numpy as np
from jax import lax

D = 2048
FF = 5632
KVH = 16
HD = 128
TOPK = 2
TOK_DEV = 128
EXP = 4
CAP = 96
NSEQ = 32
TOKENS = 4096


def draw_seq_lengths(key, part):
    key = jax.random.fold_in(key, 11)
    first_key, second_key = jax.random.split(key)
    lengths = jax.random.randint(first_key, (NSEQ,), TOK_DEV // 4, TOK_DEV + 1)
    chosen = jax.random.randint(second_key, (), 0, NSEQ)
    return jnp.where(jnp.arange(NSEQ) == chosen, TOK_DEV, lengths).astype(jnp.int32)


def steps_of(stream_key, shape, cuts, low, top_value):
    gain = 1.0
    for dim, shards_of in cuts:
        heights = jax.random.uniform(jax.random.fold_in(jax.random.fold_in(stream_key, 6), dim), (shards_of,), jnp.float32, low / len(cuts), top_value / len(cuts))
        gain = gain * jnp.repeat(jnp.exp(heights), shape[dim] // shards_of).reshape((-1,) + (1,) * (len(shape) - 1 - dim))
    return gain


def assign_block(own_key, own, number, rows, count, top, limit, slope):
    order = jax.random.permutation(own_key, count)
    packed, common = portions_of(count, rows * top, limit, slope, True), portions_of(count, rows * top, limit, slope, False)
    places = jnp.arange(count)

    def named(sizes, rotation):
        used = int((sizes > 0).sum())
        fixed = max(1, used // 4)
        moved = fixed + (places - fixed + rotation * (used - fixed)) % max(1, count - fixed)
        return jnp.zeros((count,), jnp.int32).at[order[jnp.where(places < fixed, places, moved)]].set(jnp.asarray(sizes, jnp.int32))

    sizes = jnp.where(number % 4 == 0, named(packed, number // 4), named(common, number - number // 4 - 1))
    mixed = jax.random.permutation(jax.random.fold_in(own, 3), count)
    donor, sink = mixed[0:count // 2 * 2:2], mixed[1:count // 2 * 2:2]
    room = jnp.minimum(sizes[donor] - 1, limit - sizes[sink]) // 2
    room = jnp.where((donor == order[0]) | (sink == order[0]) | (sizes[sink] == 0), 0, jnp.maximum(room, 0))
    moved = jax.random.randint(jax.random.fold_in(own, 4), (count // 2,), 0, 1 << 20) % (room + 1)
    sizes = sizes.at[donor].add(-moved).at[sink].add(moved)
    members = jnp.searchsorted(jnp.cumsum(sizes), jnp.arange(rows * top), side="right").astype(jnp.int32)
    listing = members.reshape(top, rows).T
    listing = listing[jax.random.permutation(jax.random.fold_in(own, 1), rows)]
    rotation = jax.random.randint(jax.random.fold_in(own, 2), (rows, 1), 0, top)
    return jnp.take_along_axis(listing, (jnp.arange(top)[None, :] + rotation) % top, axis=1)


def portions_of(amount, total, most, lean, full):
    portions = [(1 << 20) // math.isqrt(rank ** lean) + 1 for rank in range(1, amount + 1)]
    largest = most if full else min(most, max(-(-total // amount), total * portions[0] // sum(portions)))
    least = 1 if total - largest >= amount - 1 else 0
    counts, spare = [largest] + [least] * (amount - 1), total - largest - least * (amount - 1)
    while spare > 0:
        free = [i for i in range(1, amount) if counts[i] < largest] or [i for i in range(1, amount) if counts[i] < most]
        whole, left = sum([portions[i] for i in free]), spare
        for i in free:
            extra = min(most - counts[i], max(1, left * portions[i] // whole), spare)
            counts[i] = counts[i] + extra
            spare = spare - extra
    return np.array(counts)


def scatter_about(stream_key, dims, deviation, bound, cuts=(), kind=jnp.bfloat16):
    drawn = jax.random.normal(stream_key, dims, jnp.float32) * deviation
    if len(cuts) > 0:
        drawn = steps_of(stream_key, dims, cuts, -0.22, 0.18) * drawn
    return jnp.clip(drawn, min=-bound, max=bound).astype(kind)


def setup_inputs(seed: int = 0) -> dict:
    seeds = jax.random.split(jax.random.key(seed), 15)
    hidden_in = scatter_about(seeds[0], (TOKENS, D), 1.0, 6.0, ((0, 32),))
    seq_lengths = draw_seq_lengths(jax.random.fold_in(seeds[14], 71), 0)
    attn_routes_keys = jax.random.split(jax.random.fold_in(seeds[2], 1), TOKENS // TOK_DEV)
    attn_routes_turns = jax.random.permutation(jax.random.fold_in(seeds[2], 3), TOKENS // TOK_DEV)
    attn_routes = jax.vmap(lambda own, number: assign_block(jax.random.fold_in(seeds[2], 2), own, number, TOK_DEV, EXP, TOPK, CAP, 1))(attn_routes_keys, attn_routes_turns).reshape((TOKENS, TOPK))
    attn_gates = jnp.clip(0.25 + 0.75 * jax.random.uniform(seeds[3], (TOKENS, TOPK), jnp.float32) ** steps_of(seeds[3], (TOKENS, TOPK), ((0, 32),), -0.2, 0.2), 0.25, 1.0)
    mlp_routes_keys = jax.random.split(jax.random.fold_in(seeds[4], 1), TOKENS // TOK_DEV)
    mlp_routes_turns = jax.random.permutation(jax.random.fold_in(seeds[4], 3), TOKENS // TOK_DEV)
    mlp_routes = jax.vmap(lambda own, number: assign_block(jax.random.fold_in(seeds[4], 2), own, number, TOK_DEV, EXP, TOPK, CAP, 2))(mlp_routes_keys, mlp_routes_turns).reshape((TOKENS, TOPK))
    mlp_gates = jnp.clip(0.25 + 0.75 * jax.random.uniform(seeds[5], (TOKENS, TOPK), jnp.float32) ** steps_of(seeds[5], (TOKENS, TOPK), ((0, 32),), -0.2, 0.2), 0.25, 1.0)
    attn_gain = jnp.clip(1.0 + 0.1 * jax.random.normal(seeds[6], (D,), jnp.float32), 0.5, 1.5).astype(jnp.bfloat16)
    mlp_gain = jnp.clip(1.0 + 0.1 * jax.random.normal(seeds[7], (D,), jnp.float32), 0.5, 1.5).astype(jnp.bfloat16)
    k_weight = scatter_about(seeds[8], (KVH * HD, D), D ** -0.5, 0.125, ((0, 32),))
    v_weight = scatter_about(seeds[9], (KVH * HD, D), D ** -0.5, 0.125, ((0, 32),))
    attn_experts = scatter_about(seeds[10], (EXP, KVH * HD, 2, D), (D // 4) ** -0.5, 0.25, ((0, 4), (1, 8)))
    mlp_experts = scatter_about(seeds[11], (EXP, FF, 3, D), D ** -0.5, 0.125, ((0, 4), (1, 8)))
    logit_limit = jnp.clip(jax.random.uniform(seeds[12], (KVH,), jnp.float32, 1.5, 4.5), 1.5, 4.5)
    out_grad = scatter_about(seeds[13], (TOKENS, D), 1.0, 6.0, ((0, 32),))
    return {"hidden_in": hidden_in, "seq_lengths": seq_lengths, "attn_routes": attn_routes, "attn_gates": attn_gates, "mlp_routes": mlp_routes, "mlp_gates": mlp_gates, "attn_gain": attn_gain, "mlp_gain": mlp_gain, "k_weight": k_weight, "v_weight": v_weight, "attn_experts": attn_experts, "mlp_experts": mlp_experts, "logit_limit": logit_limit, "out_grad": out_grad}


eps = 1e-06
rope_base = 10000.0
masked_value = -1e+30
highest = lax.Precision.HIGHEST

@jax.custom_vjp
def low(v):
    return lax.optimization_barrier(v.astype(jnp.bfloat16)).astype(jnp.float32)

@jax.custom_vjp
def low_back(v):
    return v

def low_keep(v):
    return (low(v), None)

def low_pass(kept, grad):
    return (grad,)

def back_keep(v):
    return (v, None)

def back_low(kept, grad):
    return (low(grad),)
low.defvjp(low_keep, low_pass)
low_back.defvjp(back_keep, back_low)

def rms_norm(values, gain_vec):
    return values * lax.rsqrt(lax.optimization_barrier(jnp.mean(values * values, axis=-1, keepdims=True)) + eps) * gain_vec

def rotate(values, places):
    half_dim = values.shape[-1] // 2
    freqs = rope_base ** (-jnp.arange(half_dim, dtype=jnp.float32) / half_dim)
    angles = places.astype(jnp.float32)[..., None, None] * freqs
    cosine = jnp.cos(angles)
    sine_val = jnp.sin(angles)
    first_half = values[..., :half_dim]
    second_half = values[..., half_dim:]
    return jnp.concatenate([first_half * cosine - second_half * sine_val, second_half * cosine + first_half * sine_val], axis=-1)

def tables(routes, gate_vals, length, expert_count, slot_cap):
    seq_len = routes.shape[0]
    choices_per = routes.shape[1]
    flat_ids = routes.reshape(-1)
    places = jnp.arange(seq_len, dtype=jnp.int32)
    labels = jnp.arange(expert_count, dtype=jnp.int32)
    onehot = (flat_ids[:, None] == labels[None, :]).astype(jnp.int32)
    ranking = lax.optimization_barrier(jnp.sum((jnp.cumsum(onehot, axis=0) - onehot) * onehot, axis=1))
    slot_ids = jnp.arange(slot_cap, dtype=jnp.int32)
    is_live = jnp.repeat(places < length, choices_per)
    matches = (flat_ids[None, None, :] == labels[:, None, None]) & (ranking[None, None, :] == slot_ids[None, :, None]) & is_live[None, None, :]
    matches = matches.reshape(expert_count, slot_cap, seq_len, choices_per).astype(jnp.int32)
    taken_rows = lax.optimization_barrier(jnp.sum(matches, axis=3))
    slot_place = lax.optimization_barrier(jnp.sum(taken_rows * places[None, None, :], axis=2))
    filled = lax.optimization_barrier(jnp.sum(taken_rows, axis=2))
    weighted = lax.optimization_barrier(jnp.sum(matches.astype(jnp.float32) * gate_vals[None, None, :, :], axis=3))
    return (taken_rows.astype(jnp.float32), weighted, slot_place, filled)

def reference(hidden_in, seq_lengths, attn_routes, attn_gates, mlp_routes, mlp_gates, attn_gain, mlp_gain, k_weight, v_weight, attn_experts, mlp_experts, logit_limit, out_grad):
    build_tables = jax.vmap(lambda routes, gate_vals, length: tables(routes, gate_vals, length, EXP, CAP))
    attn_tab = build_tables(attn_routes.reshape(NSEQ, TOK_DEV, TOPK), attn_gates.reshape(NSEQ, TOK_DEV, TOPK), seq_lengths)
    mlp_tab = build_tables(mlp_routes.reshape(NSEQ, TOK_DEV, TOPK), mlp_gates.reshape(NSEQ, TOK_DEV, TOPK), seq_lengths)
    groups = NSEQ // 8
    score_scale = HD ** (-0.5)

    def by_groups(values):
        return values.reshape((groups, 8) + values.shape[1:])
    fixed_parts = (by_groups(seq_lengths), by_groups(attn_tab[0]), by_groups(attn_tab[1]), by_groups(attn_tab[2]), by_groups(attn_tab[3]), by_groups(mlp_tab[0]), by_groups(mlp_tab[1]))

    def forward(hidden, k_w, v_w, gain_one, gain_two, attn_w, mlp_w):

        def group_block(group_piece):
            source, lengths, attn_disp, attn_comb, attn_place, attn_fill, mlp_disp, mlp_comb = group_piece
            places = jnp.arange(TOK_DEV, dtype=jnp.int32)
            keep_mask = (places[None, :] < lengths[:, None]).astype(jnp.float32)[..., None]
            norm_one = low(rms_norm(source, gain_one))
            key_raw = low_back(jnp.einsum('gsd,fd->gsf', norm_one, k_w, precision=highest))
            key_rows = low(rotate(key_raw.reshape(8, TOK_DEV, KVH, HD), jnp.broadcast_to(places, (8, TOK_DEV))))
            val_rows = low(low_back(jnp.einsum('gsd,fd->gsf', norm_one, v_w, precision=highest))).reshape(8, TOK_DEV, KVH, HD)
            attn_rows = low_back(jnp.einsum('gecs,gsd->gecd', attn_disp, norm_one, precision=highest))
            query_raw = low_back(jnp.einsum('gecd,efd->gecf', attn_rows, attn_w[:, :, 0, :], precision=highest))
            queries = low(rotate(query_raw.reshape(8, EXP, CAP, KVH, HD), attn_place))
            scores = low_back(jnp.einsum('gechk,gshk->gehcs', queries, key_rows, precision=highest) * score_scale)
            allowed = (places[None, None, None, :] <= attn_place[..., None]) & (places[None, None, None, :] < lengths[:, None, None, None])
            allowed = allowed[:, :, None]
            masked = jnp.where(allowed, scores, masked_value)
            shifted = jnp.exp(masked - lax.optimization_barrier(jnp.max(masked, axis=-1, keepdims=True)))
            prob_low = low(shifted / lax.optimization_barrier(jnp.sum(shifted, axis=-1, keepdims=True)))
            mixed_heads = low_back(low(jnp.einsum('gehcs,gshk->gechk', prob_low, val_rows, precision=highest))).reshape(8, EXP, CAP, KVH * HD)
            attn_result = low_back(low(jnp.einsum('gecf,efd->gecd', mixed_heads, attn_w[:, :, 1, :], precision=highest)))
            attn_out = jnp.einsum('gecs,gecd->gsd', attn_comb, attn_result, precision=highest)
            middle = source + attn_out
            norm_two = low(rms_norm(middle, gain_two))
            mlp_rows = low_back(jnp.einsum('gecs,gsd->gecd', mlp_disp, norm_two, precision=highest))
            gate_pre = low_back(jnp.einsum('gecd,efd->gecf', mlp_rows, mlp_w[:, :, 0, :], precision=highest))
            up_pre = low_back(jnp.einsum('gecd,efd->gecf', mlp_rows, mlp_w[:, :, 1, :], precision=highest))
            units = low(jax.nn.silu(gate_pre) * up_pre)
            mlp_result = low_back(low(jnp.einsum('gecf,efd->gecd', units, mlp_w[:, :, 2, :], precision=highest)))
            mlp_out = jnp.einsum('gecs,gecd->gsd', mlp_comb, mlp_result, precision=highest)
            result = keep_mask * (middle + mlp_out)
            live_rows = (attn_fill > 0)[:, :, None, :, None]
            peak_logit = lax.optimization_barrier(jnp.max(jnp.where(allowed & live_rows, scores, masked_value), axis=(0, 1, 3, 4)))
            return (result, peak_logit)
        results, peaks = lax.map(jax.checkpoint(group_block), (by_groups(hidden),) + fixed_parts)
        return (results.reshape(TOKENS, D), lax.optimization_barrier(jnp.max(peaks, axis=0)))
    primal, pull_back, peak_all = jax.vjp(forward, hidden_in.reshape(NSEQ, TOK_DEV, D).astype(jnp.float32), k_weight.astype(jnp.float32), v_weight.astype(jnp.float32), attn_gain.astype(jnp.float32), mlp_gain.astype(jnp.float32), attn_experts.astype(jnp.float32), mlp_experts.astype(jnp.float32), has_aux=True)
    gradient = pull_back(out_grad.astype(jnp.float32))
    factors = logit_limit / jnp.maximum(peak_all, logit_limit)
    row_scale = jnp.repeat(jnp.sqrt(factors), HD)
    clipped_query = (attn_experts[:, :, 0, :].astype(jnp.float32) * row_scale[None, :, None]).astype(jnp.bfloat16)
    clipped_key = (k_weight.astype(jnp.float32) * row_scale[:, None]).astype(jnp.bfloat16)
    return (primal.astype(jnp.bfloat16), gradient[0].reshape(TOKENS, D), gradient[1], gradient[2], gradient[3], gradient[4], gradient[5], gradient[6], clipped_query, clipped_key, factors)
```

```python
import functools

import jax
import jax.numpy as jnp
from jax import lax
from jax.experimental import pallas as pl
from jax.experimental.pallas import tpu as pltpu
from jax.sharding import PartitionSpec as P

HD = 128
eps = 1e-06
rope_base = 10000.0
masked_value = -1e30
f32 = jnp.float32
bf16 = jnp.bfloat16


def rms_inverse(values):
    return lax.rsqrt(jnp.mean(values * values, axis=-1, keepdims=True) + eps)


def norm_back(values, gain_vec, grad_out):
    inverse = rms_inverse(values)
    scaled = grad_out * gain_vec
    inner = jnp.mean(scaled * values, axis=-1, keepdims=True)
    grad_values = inverse * scaled - values * inverse * inverse * inverse * inner
    grad_gain = jnp.sum(grad_out * values * inverse, axis=0)
    return (grad_values, grad_gain)


def dot_nt(left, right):
    return lax.dot_general(left, right, (((1,), (1,)), ((), ())), preferred_element_type=f32)


def dot_nn(left, right):
    return lax.dot_general(left, right, (((1,), (0,)), ((), ())), preferred_element_type=f32)


def dot_tn(left, right):
    return lax.dot_general(left, right, (((0,), (0,)), ((), ())), preferred_element_type=f32)


def two_parts(values):
    high = values.astype(bf16)
    return high, (values - high.astype(f32)).astype(bf16)


class Plain:
    def __init__(self, mesh):
        self.pair = 1
        self.tp = mesh.shape["dp"]
        self.experts = mesh.shape["expert"]

    def labels(self):
        return jnp.arange(self.experts, dtype=jnp.int32)

    def spread(self, blocks):
        moved = lax.all_to_all(jnp.stack(blocks), "expert", 0, 0, tiled=True)
        return [lax.all_gather(one, "dp", axis=0, tiled=True) for one in moved]

    spread_small = spread

    def collect(self, parts):
        mine = [
            lax.psum_scatter(one.astype(bf16), "dp", scatter_dimension=0, tiled=True)
            for one in parts
        ]
        moved = lax.all_to_all(jnp.stack(mine), "expert", 0, 0, tiled=True)
        return [one for one in moved]

    def gather_all(self, block):
        rows = lax.all_gather(block, "expert", axis=0, tiled=False)
        return [lax.all_gather(one, "dp", axis=0, tiled=True) for one in rows]

    def reduce_all(self, parts):
        mine = [
            lax.psum_scatter(one.astype(bf16), "dp", scatter_dimension=0, tiled=True)
            for one in parts
        ]
        total = lax.psum_scatter(jnp.stack(mine), "expert", scatter_dimension=0, tiled=True)
        return total[0].astype(f32)

    def pair_gather(self, block):
        return block

    def pair_scatter(self, part):
        return part

    def column_gather(self, block):
        return lax.all_gather(block, "expert", axis=0, tiled=False)[None]

    def column_scatter(self, part):
        return lax.psum_scatter(
            part[0].astype(bf16), "expert", scatter_dimension=0, tiled=True
        )[0].astype(f32)

    def gather_vec(self, block):
        return lax.all_gather(block, ("dp", "expert"), axis=1, tiled=True)

    def sum_vec(self, vec):
        return lax.psum_scatter(vec, ("dp", "expert"), scatter_dimension=1, tiled=True)

    def max_vec(self, vec):
        return lax.pmax(vec, ("dp", "expert"))


def swap(block, mask):
    return lax.ppermute(block, "dp", [(i, i ^ mask) for i in range(8)])


def flip(block, mask):
    return lax.ppermute(block, "expert", [(i, i ^ mask) for i in range(4)])


def hop(block, pairs):
    return lax.ppermute(block, "expert", pairs)


CORE, SIDE_X, SIDE_Y = 1, 2, 4
INWARD = [(0, 1), (3, 2)]
OUTWARD = [(1, 0), (2, 3)]
MIDDLE = [(1, 2), (2, 1)]


class Paired:
    def __init__(self, mesh):
        self.pair = 2
        self.tp = 4
        self.experts = 4

    def labels(self):
        return lax.axis_index("expert") ^ jnp.arange(4, dtype=jnp.int32)

    def plane_gather(self, block):
        half = block.shape[0] // 2
        from_x = swap(block, SIDE_X)
        from_y = swap(block, SIDE_Y)
        low = swap(from_y[:half], SIDE_X)
        high = swap(from_x[half:], SIDE_Y)
        return jnp.concatenate([block, from_x, from_y, low, high], axis=0)

    def plane_reduce(self, part):
        size = part.shape[0] // 4
        half = size // 2
        own, to_x, to_y, across = (part[i * size : (i + 1) * size] for i in range(4))
        across = across.astype(bf16)
        low = swap(across[:half], SIDE_X)
        high = swap(across[half:], SIDE_Y)
        to_y = jnp.concatenate([to_y[:half] + low.astype(f32), to_y[half:]], axis=0)
        to_x = jnp.concatenate([to_x[:half], to_x[half:] + high.astype(f32)], axis=0)
        from_x = swap(to_x.astype(bf16), SIDE_X)
        from_y = swap(to_y.astype(bf16), SIDE_Y)
        return own + from_x.astype(f32) + from_y.astype(f32)

    def line_gather(self, block):
        near = flip(block, 1)
        crossed = hop(block, MIDDLE)
        second = hop(crossed, OUTWARD) + hop(near, MIDDLE)
        third = crossed + hop(second, OUTWARD)
        return [block, near, second, third]

    def line_reduce(self, parts):
        own, near, second, third = parts
        second = second + hop(third.astype(bf16), INWARD).astype(f32)
        second = second.astype(bf16)
        third = third + hop(second, INWARD).astype(f32)
        near = near + hop(second, MIDDLE).astype(f32)
        return (
            own
            + flip(near.astype(bf16), 1).astype(f32)
            + hop(third.astype(bf16), MIDDLE).astype(f32)
        )

    def reorder(self, parts):
        place = lax.axis_index("expert")
        odd = (place & 1) == 1
        parts = [jnp.where(odd, parts[i ^ 1], parts[i]) for i in range(4)]
        upper = (place & 2) == 2
        return [jnp.where(upper, parts[i ^ 2], parts[i]) for i in range(4)]

    def spread(self, blocks):
        return [
            self.plane_gather(one if r == 0 else flip(one, r)) for r, one in enumerate(blocks)
        ]

    def spread_small(self, blocks):
        moved = jnp.concatenate(
            [one if r == 0 else flip(one, r) for r, one in enumerate(blocks)], axis=0
        )
        quads = jnp.stack([moved] + [swap(moved, mask) for mask in (2, 4, 6)], axis=1)
        return [one for one in quads]

    def collect(self, parts):
        mine = [self.plane_reduce(one).astype(bf16) for one in parts]
        return [one if r == 0 else flip(one, r) for r, one in enumerate(mine)]

    def gather_all(self, block):
        return [self.plane_gather(one) for one in self.line_gather(block)]

    def reduce_all(self, parts):
        return self.line_reduce([self.plane_reduce(one) for one in parts])

    def pair_gather(self, block):
        return jnp.concatenate([block, swap(block, CORE)], axis=0)

    def pair_scatter(self, part):
        size = part.shape[0] // 2
        return part[:size] + swap(part[size:].astype(bf16), CORE).astype(f32)

    def column_gather(self, block):
        mine = jnp.stack(self.reorder(self.line_gather(block)))
        return jnp.stack([mine, swap(mine, CORE)])

    def column_scatter(self, part):
        mine = part[0] + swap(part[1].astype(bf16), CORE).astype(f32)
        return self.line_reduce(self.reorder([mine[i] for i in range(4)]))

    def butterfly(self, vec, merge):
        for mask in (CORE, SIDE_X, SIDE_Y):
            vec = merge(vec, swap(vec, mask))
        for mask in (1, 2):
            vec = merge(vec, flip(vec, mask))
        return vec

    def gather_vec(self, block):
        place = lax.axis_index("dp") * 4 + lax.axis_index("expert")
        owner = (jnp.arange(32, dtype=jnp.int32) == place)[None, :, None]
        spread = jnp.where(owner, block[:, None, :], jnp.zeros_like(block)[:, None, :])
        return self.butterfly(spread.reshape(block.shape[0], -1), jnp.add)

    def sum_vec(self, vec):
        place = lax.axis_index("dp") * 4 + lax.axis_index("expert")
        total = self.butterfly(vec, jnp.add)
        size = vec.shape[1] // 32
        return lax.dynamic_slice_in_dim(total, place * size, size, 1)

    def max_vec(self, vec):
        return self.butterfly(vec, jnp.maximum)


def turn(values, cosine, sine):
    return values * cosine + pltpu.roll(values, HD // 2, 1) * sine


def causal_mask(size):
    keys = lax.broadcasted_iota(jnp.int32, (size, size), 0)
    queries = lax.broadcasted_iota(jnp.int32, (size, size), 1)
    return keys <= queries


def slot_rows(cap, index):
    slots = lax.broadcasted_iota(jnp.int32, (cap, index.shape[1]), 0)
    return (slots == index).astype(f32).astype(bf16)


def attend_kernel(
    heads, scale, raw_ref, cos_ref, sin_ref, idx_ref, qkv_ref, mixed_ref, peak_ref
):
    size = raw_ref.shape[0]
    wide = heads * HD
    cap = mixed_ref.shape[0]
    cosine, sine = cos_ref[...], sin_ref[...]
    index = idx_ref[0]
    causal = causal_mask(size)
    mixed = []
    for h in range(heads):
        q_at = slice(h * HD, (h + 1) * HD)
        k_at = slice(wide + h * HD, wide + (h + 1) * HD)
        v_at = slice(2 * wide + h * HD, 2 * wide + (h + 1) * HD)
        query = turn(raw_ref[:, q_at], cosine, sine).astype(bf16)
        key = turn(raw_ref[:, k_at], cosine, sine).astype(bf16)
        value = raw_ref[:, v_at].astype(bf16)
        qkv_ref[:, q_at] = query
        qkv_ref[:, k_at] = key
        qkv_ref[:, v_at] = value
        scores = jnp.where(causal, dot_nt(key, query) * scale, masked_value)
        top = jnp.max(scores, axis=0, keepdims=True)
        peak_ref[0, h : h + 1, :] = jnp.where(index >= 0, top, masked_value)
        shifted = jnp.exp(scores - top)
        prob = (shifted / jnp.sum(shifted, axis=0, keepdims=True)).astype(bf16)
        mixed.append(dot_tn(prob, value).astype(bf16))
    mixed_ref[...] = dot_nn(slot_rows(cap, index), jnp.concatenate(mixed, axis=1)).astype(bf16)


def attend(raw, cosine, sine, index, cap):
    seqs, size = index.shape
    wide = raw.shape[1] // 3
    heads = wide // HD
    table = pl.BlockSpec((size, HD), lambda s: (0, 0))
    return pl.pallas_call(
        functools.partial(attend_kernel, heads, HD ** (-0.5)),
        grid=(seqs,),
        in_specs=[
            pl.BlockSpec((size, 3 * wide), lambda s: (s, 0)),
            table,
            table,
            pl.BlockSpec((1, 1, size), lambda s: (s, 0, 0)),
        ],
        out_specs=[
            pl.BlockSpec((size, 3 * wide), lambda s: (s, 0)),
            pl.BlockSpec((cap, wide), lambda s: (s, 0)),
            pl.BlockSpec((1, heads, size), lambda s: (s, 0, 0)),
        ],
        out_shape=[
            jax.ShapeDtypeStruct((seqs * size, 3 * wide), bf16),
            jax.ShapeDtypeStruct((seqs * cap, wide), bf16),
            jax.ShapeDtypeStruct((seqs, heads, size), f32),
        ],
        cost_estimate=pl.CostEstimate(
            flops=seqs * heads * size * size * HD * 6,
            bytes_accessed=seqs * size * wide * 20,
            transcendentals=seqs * heads * size * size,
        ),
        name="attend",
    )(raw, cosine, sine, index[:, None, :])


def attend_back_kernel(heads, scale, qkv_ref, gm_ref, cos_ref, sin_ref, idx_ref, out_ref):
    size = qkv_ref.shape[0]
    wide = heads * HD
    cap = gm_ref.shape[0]
    cosine, sine = cos_ref[...], -sin_ref[...]
    causal = causal_mask(size)
    grad_mixed = dot_tn(slot_rows(cap, idx_ref[0]), gm_ref[...]).astype(bf16)
    for h in range(heads):
        q_at = slice(h * HD, (h + 1) * HD)
        k_at = slice(wide + h * HD, wide + (h + 1) * HD)
        v_at = slice(2 * wide + h * HD, 2 * wide + (h + 1) * HD)
        query, key, value = qkv_ref[:, q_at], qkv_ref[:, k_at], qkv_ref[:, v_at]
        grad = grad_mixed[:, q_at]
        scores = jnp.where(causal, dot_nt(key, query) * scale, masked_value)
        top = jnp.max(scores, axis=0, keepdims=True)
        shifted = jnp.exp(scores - top)
        prob = shifted / jnp.sum(shifted, axis=0, keepdims=True)
        grad_prob = dot_nt(value, grad)
        inner = jnp.sum(prob * grad_prob, axis=0, keepdims=True)
        grad_scores = (prob * (grad_prob - inner)).astype(bf16)
        grad_query = dot_tn(grad_scores, key) * scale
        grad_key = dot_nn(grad_scores, query) * scale
        out_ref[:, q_at] = turn(grad_query, cosine, sine).astype(bf16)
        out_ref[:, k_at] = turn(grad_key, cosine, sine).astype(bf16)
        out_ref[:, v_at] = dot_nn(prob.astype(bf16), grad).astype(bf16)


def attend_back(qkv, grad_mixed, cosine, sine, index):
    seqs, size = index.shape
    cap = grad_mixed.shape[0] // seqs
    wide = qkv.shape[1] // 3
    heads = wide // HD
    table = pl.BlockSpec((size, HD), lambda s: (0, 0))
    return pl.pallas_call(
        functools.partial(attend_back_kernel, heads, HD ** (-0.5)),
        grid=(seqs,),
        in_specs=[
            pl.BlockSpec((size, 3 * wide), lambda s: (s, 0)),
            pl.BlockSpec((cap, wide), lambda s: (s, 0)),
            table,
            table,
            pl.BlockSpec((1, 1, size), lambda s: (s, 0, 0)),
        ],
        out_specs=pl.BlockSpec((size, 3 * wide), lambda s: (s, 0)),
        out_shape=jax.ShapeDtypeStruct((seqs * size, 3 * wide), bf16),
        cost_estimate=pl.CostEstimate(
            flops=seqs * heads * size * size * HD * 12,
            bytes_accessed=seqs * size * wide * 14,
            transcendentals=seqs * heads * size * size,
        ),
        name="attend_back",
    )(qkv, grad_mixed, cosine, sine, index[:, None, :])


def on_device(
    links,
    hidden_in,
    seq_lengths,
    attn_routes,
    attn_gates,
    mlp_routes,
    mlp_gates,
    attn_gain,
    mlp_gain,
    k_weight,
    v_weight,
    attn_experts,
    mlp_experts,
    logit_limit,
    out_grad,
):
    experts = links.experts
    seq_len, width = hidden_in.shape
    cap = seq_len * attn_routes.shape[1] * 3 // (2 * experts)
    shard_heads = attn_experts.shape[1] // HD
    local_heads = shard_heads * links.pair
    wide = local_heads * HD
    dp_id = lax.axis_index("dp")
    places = jnp.arange(seq_len, dtype=jnp.int32)
    live = places < seq_lengths[0]
    labels = links.labels()

    hidden_chunks = links.gather_all(hidden_in)
    gains = links.gather_vec(jnp.stack([attn_gain, mlp_gain])).astype(f32)
    gain_first, gain_second = gains[0:1], gains[1:2]
    key_value = links.column_gather(jnp.concatenate([k_weight, v_weight], axis=0))
    key_rows = k_weight.shape[0]
    k_local = key_value[:, :, :key_rows].reshape(wide, width)
    v_local = key_value[:, :, key_rows:].reshape(wide, width)
    q_local = links.pair_gather(attn_experts[0, :, 0, :])
    o_local = links.pair_gather(attn_experts[0, :, 1, :])
    qkv_w = jnp.concatenate([q_local, k_local, v_local], axis=0)
    gate_w = links.pair_gather(mlp_experts[0, :, 0, :])
    up_w = links.pair_gather(mlp_experts[0, :, 1, :])
    down_w = links.pair_gather(mlp_experts[0, :, 2, :])

    before = (places[:, None] < places[None, :]).astype(bf16)

    def slot_tables(routes, gates):
        first, second = routes[:, 0][None, :], routes[:, 1][None, :]
        names = labels[:, None]
        named = (first == names) | (second == names)
        rank = dot_nn(named.astype(bf16), before).astype(jnp.int32)
        index = jnp.where(named & live[None, :], rank, -1)
        weight = jnp.where(first == names, gates[:, 0][None, :], 0.0) + jnp.where(
            second == names, gates[:, 1][None, :], 0.0
        )
        slot_ids = jnp.arange(cap, dtype=jnp.int32)[None, :, None]
        taken = slot_ids == index[:, None, :]
        combine = jnp.where(taken, weight[:, None, :], 0.0)
        slot_gate = jnp.sum(combine, axis=2)[:, :, None]
        taken = taken.astype(bf16)
        return index, taken, slot_gate, two_parts(combine)

    attn_index, attn_taken, attn_slot_gate, attn_combine = slot_tables(attn_routes, attn_gates)
    _, mlp_taken, mlp_slot_gate, mlp_combine = slot_tables(mlp_routes, mlp_gates)
    index_chunks = links.spread_small([attn_index[r : r + 1] for r in range(experts)])

    def combine_rows(parts, rows):
        rows = jnp.concatenate(rows, axis=0)
        flat = [one.reshape(experts * cap, seq_len) for one in parts]
        return sum(dot_tn(one, rows) for one in flat)

    grad_slots = [
        (mlp_slot_gate[r] * dot_nn(mlp_taken[r], out_grad)).astype(bf16) for r in range(experts)
    ]
    grad_rows = links.spread(grad_slots)

    half = HD // 2
    freqs = rope_base ** (-jnp.arange(half, dtype=f32) / half)
    angles = places.astype(f32)[:, None] * freqs[None, :]
    cosine = jnp.concatenate([jnp.cos(angles), jnp.cos(angles)], axis=1)
    sine = jnp.concatenate([-jnp.sin(angles), jnp.sin(angles)], axis=1)

    normed, turned, mixed_rows, peaks, attn_parts = [], [], [], [], []
    for r in range(experts):
        values = hidden_chunks[r].astype(f32)
        norm_one = (values * rms_inverse(values) * gain_first).astype(bf16)
        raw = dot_nt(norm_one, qkv_w)
        qkv, mixed, peak = attend(raw, cosine, sine, index_chunks[r], cap)
        normed.append(norm_one)
        turned.append(qkv)
        mixed_rows.append(mixed)
        peaks.append(jnp.max(peak, axis=(0, 2)))
        attn_parts.append(dot_nn(mixed, o_local))
    attn_back = links.collect(attn_parts)
    hidden = hidden_in.astype(f32)
    middle = hidden + combine_rows(attn_combine, attn_back)
    norm_two = (middle * rms_inverse(middle) * gain_second).astype(bf16)
    mlp_slots = [dot_nn(mlp_taken[r], norm_two).astype(bf16) for r in range(experts)]
    mlp_rows = links.spread(mlp_slots)

    units_all, gate_all, up_all, mlp_parts, grad_parts = [], [], [], [], []
    for r in range(experts):
        grad_units = dot_nt(grad_rows[r], down_w)
        gate_pre = dot_nt(mlp_rows[r], gate_w)
        up_pre = dot_nt(mlp_rows[r], up_w)
        gate_sig = jax.nn.sigmoid(gate_pre)
        silu_val = gate_pre * gate_sig
        units = (silu_val * up_pre).astype(bf16)
        grad_gate = (grad_units * up_pre * gate_sig * (1.0 + gate_pre * (1.0 - gate_sig))).astype(
            bf16
        )
        grad_up = (grad_units * silu_val).astype(bf16)
        grad_parts.append(dot_nn(grad_gate, gate_w) + dot_nn(grad_up, up_w))
        mlp_parts.append(dot_nn(units, down_w))
        units_all.append(units)
        gate_all.append(grad_gate)
        up_all.append(grad_up)
    grad_back = links.collect(grad_parts)
    mlp_back = links.collect(mlp_parts)

    keep = live.astype(f32)[:, None]
    block_out = (keep * (middle + combine_rows(mlp_combine, mlp_back))).astype(bf16)
    grad_norm_two = combine_rows([mlp_taken], grad_back)
    grad_mid_norm, gain_two_grad = norm_back(middle, gain_second, grad_norm_two)
    grad_middle = out_grad.astype(f32) * keep + grad_mid_norm
    mid_high, mid_low = two_parts(grad_middle)
    attn_grad_slots = [
        (
            attn_slot_gate[r]
            * (dot_nn(attn_taken[r], mid_high) + dot_nn(attn_taken[r], mid_low))
        ).astype(bf16)
        for r in range(experts)
    ]
    attn_grad_rows = links.spread(attn_grad_slots)

    grads_all, norm_parts = [], []
    for r in range(experts):
        grad_mixed = dot_nt(attn_grad_rows[r], o_local).astype(bf16)
        grads = attend_back(turned[r], grad_mixed, cosine, sine, index_chunks[r])
        norm_parts.append(dot_nn(grads, qkv_w))
        grads_all.append(grads)
    grad_norm_one = links.reduce_all(norm_parts)

    def joined(parts):
        return jnp.concatenate(parts, axis=0)

    rows_all, grad_rows_all = joined(mlp_rows), joined(grad_rows)
    mlp_grad = jnp.stack(
        [
            links.pair_scatter(dot_tn(joined(gate_all), rows_all)),
            links.pair_scatter(dot_tn(joined(up_all), rows_all)),
            links.pair_scatter(dot_tn(joined(units_all), grad_rows_all)),
        ],
        axis=1,
    )[None]
    qkv_grad = dot_tn(joined(grads_all), joined(normed))
    attn_grad = jnp.stack(
        [
            links.pair_scatter(qkv_grad[:wide]),
            links.pair_scatter(dot_tn(joined(mixed_rows), joined(attn_grad_rows))),
        ],
        axis=1,
    )[None]
    column = (links.pair, experts, key_rows, width)
    kv_grad = links.column_scatter(
        jnp.concatenate(
            [qkv_grad[wide : 2 * wide].reshape(column), qkv_grad[2 * wide :].reshape(column)],
            axis=2,
        )
    )
    k_grad, v_grad = kv_grad[:key_rows], kv_grad[key_rows:]

    grad_hid_norm, gain_one_grad = norm_back(hidden, gain_first, grad_norm_one)
    grad_input = grad_middle + grad_hid_norm
    gain_grads = links.sum_vec(jnp.stack([gain_one_grad, gain_two_grad]))

    head_count = logit_limit.shape[0]
    local_peak = jnp.max(jnp.stack(peaks), axis=0)
    owners = jnp.concatenate(
        [(dp_id ^ i) * shard_heads + jnp.arange(shard_heads) for i in range(links.pair)]
    )
    spots = owners[:, None] == jnp.arange(head_count)[None, :]
    peak_vec = jnp.max(jnp.where(spots, local_peak[:, None], masked_value), axis=0)
    factors = logit_limit / jnp.maximum(links.max_vec(peak_vec), logit_limit)
    roots = jnp.sqrt(factors)

    def row_scale(first_row, count):
        rows = first_row + jnp.arange(count, dtype=jnp.int32)
        heads = (rows // HD)[:, None] == jnp.arange(head_count)[None, :]
        return jnp.sum(jnp.where(heads, roots[None, :], 0.0), axis=1, keepdims=True)

    query_count = attn_experts.shape[1]
    clipped_query = (
        attn_experts[0, :, 0, :].astype(f32) * row_scale(dp_id * query_count, query_count)
    ).astype(bf16)[None]
    device_id = dp_id * experts + lax.axis_index("expert")
    clipped_key = (
        k_weight.astype(f32) * row_scale(device_id * key_rows, key_rows)
    ).astype(bf16)
    return (
        block_out,
        grad_input,
        k_grad,
        v_grad,
        gain_grads[0],
        gain_grads[1],
        attn_grad,
        mlp_grad,
        clipped_query,
        clipped_key,
        factors,
    )


def solution(mesh):
    paired = mesh.shape["dp"] == 8 and mesh.shape["expert"] == 4
    links = Paired(mesh) if paired else Plain(mesh)
    rows = P(("dp", "expert"), None)
    vec = P(("dp", "expert"))
    weights = P("expert", "dp", None, None)
    return jax.shard_map(
        functools.partial(on_device, links),
        mesh=mesh,
        in_specs=(rows, vec, rows, rows, rows, rows, vec, vec, rows, rows)
        + (weights, weights, P(), rows),
        out_specs=(rows, rows, rows, rows, vec, vec, weights, weights)
        + (P("expert", "dp", None), rows, P()),
        check_vma=False,
    )
```

```python
import functools

import jax
import jax.numpy as jnp
from jax import lax
from jax.experimental import pallas as pl
from jax.experimental.pallas import tpu as pltpu
from jax.sharding import PartitionSpec as P

HD = 128
eps = 1e-06
rope_base = 10000.0
masked_value = -1e30
f32 = jnp.float32
bf16 = jnp.bfloat16


def rms_inverse(values):
    return lax.rsqrt(jnp.mean(values * values, axis=-1, keepdims=True) + eps)


def norm_back(values, gain_vec, grad_out):
    inverse = rms_inverse(values)
    scaled = grad_out * gain_vec
    inner = jnp.mean(scaled * values, axis=-1, keepdims=True)
    grad_values = inverse * scaled - values * inverse * inverse * inverse * inner
    grad_gain = jnp.sum(grad_out * values * inverse, axis=0)
    return (grad_values, grad_gain)


def dot_nt(left, right):
    return lax.dot_general(left, right, (((1,), (1,)), ((), ())), preferred_element_type=f32)


def dot_nn(left, right):
    return lax.dot_general(left, right, (((1,), (0,)), ((), ())), preferred_element_type=f32)


def dot_tn(left, right):
    return lax.dot_general(left, right, (((0,), (0,)), ((), ())), preferred_element_type=f32)


def two_parts(values):
    high = values.astype(bf16)
    return high, (values - high.astype(f32)).astype(bf16)


CORE, SIDE_X, SIDE_Y = 1, 2, 4
flows = []


def spawn(flow):
    flows.append([flow, None])


def pause(steps):
    for _ in range(steps):
        yield ()


def drive():
    while flows:
        due, going = [], []
        for entry in flows:
            try:
                values = entry[0].send(entry[1])
            except StopIteration:
                continue
            going.append((entry, len(values)))
            due.extend(values)
        flows[:] = [entry for entry, _ in going]
        if due:
            due = lax.optimization_barrier(tuple(due))
        place = 0
        for entry, count in going:
            entry[1] = tuple(due[place : place + count])
            place += count


class Plain:
    def __init__(self, mesh):
        self.pair = 1
        self.column_steps = 0
        self.tp = mesh.shape["dp"]
        self.experts = mesh.shape["expert"]

    def labels(self):
        return jnp.arange(self.experts, dtype=jnp.int32)

    def order(self):
        return list(range(self.experts))

    def exchange(self, blocks):
        moved = lax.all_to_all(jnp.stack(blocks), "expert", 0, 0, tiled=True)
        moved = yield tuple(one for one in moved)
        return moved

    def order_back(self):
        return list(range(self.experts))

    def spread(self, blocks, ready, order):
        moved = yield from self.exchange(blocks)
        for r, one in enumerate(moved):
            rows = yield from self.plane_gather(one)
            ready(r, rows)

    def collect(self, parts, r, part, last=False, slow=0):
        parts[r] = yield from self.plane_reduce(part)
        if len(parts) == self.experts:
            moved = yield from self.exchange([parts[i] for i in range(self.experts)])
            return list(moved)
        return None

    def line_gather(self, block, ready):
        rows = lax.all_gather(block, "expert", axis=0, tiled=False)
        rows = yield tuple(one for one in rows)
        for r, one in enumerate(rows):
            ready(r, one)
        return rows

    def plane_gather(self, block, axes=None):
        (rows,) = yield (lax.all_gather(block, "dp", axis=0, tiled=True),)
        return rows

    def plane_reduce(self, part):
        mine = lax.psum_scatter(part.astype(bf16), "dp", scatter_dimension=0, tiled=True)
        (mine,) = yield (mine,)
        return mine

    def share(self, index, gains):
        yield ()
        moved = lax.all_to_all(index[:, None, :], "expert", 0, 0, tiled=True)
        rows = lax.all_gather(moved, "dp", axis=1, tiled=True)
        gains = lax.all_gather(gains, ("dp", "expert"), axis=1, tiled=True)
        return [one for one in rows], gains

    def pair_gather(self, block):
        (block,) = yield (block,)
        return (block,)

    def pair_scatter(self, part):
        (part,) = yield (part,)
        return part.astype(f32)

    def column_gather(self, block):
        (rows,) = yield (lax.all_gather(block, "expert", axis=0, tiled=False),)
        return (rows,)

    def column_scatter(self, part):
        total = lax.psum_scatter(
            part[0].astype(bf16), "expert", scatter_dimension=0, tiled=True
        )
        (total,) = yield (total,)
        return total[0].astype(f32)

    def totals(self, sums, peak):
        yield ()
        sums = lax.psum_scatter(sums, ("dp", "expert"), scatter_dimension=1, tiled=True)
        return sums, lax.pmax(peak, ("dp", "expert"))


def swap(block, mask):
    return lax.ppermute(block, "dp", [(i, i ^ mask) for i in range(8)])


def flip(block, mask):
    return lax.ppermute(block, "expert", [(i, i ^ mask) for i in range(4)])


class Paired:
    def __init__(self, mesh):
        self.pair = 2
        self.column_steps = 2
        self.tp = 4
        self.experts = 4

    def labels(self):
        return lax.axis_index("expert") ^ jnp.arange(4, dtype=jnp.int32)

    def plane_gather(self, block, axes=(SIDE_X, SIDE_Y), slow=0):
        other = swap(block, axes[0])
        yield from pause(slow)
        (other,) = yield (other,)
        both = jnp.concatenate([block, other], axis=0)
        other = swap(both, axes[1])
        yield from pause(slow)
        (other,) = yield (other,)
        if axes[0] == SIDE_X:
            return jnp.concatenate([both, other], axis=0)
        size = block.shape[0]
        return jnp.concatenate([block, other[:size], both[size:], other[size:]], axis=0)

    def plane_gather_even(self, block):
        half = block.shape[0] // 2
        from_x, from_y = yield (swap(block, SIDE_X), swap(block, SIDE_Y))
        low, high = yield (swap(from_y[:half], SIDE_X), swap(from_x[half:], SIDE_Y))
        return jnp.concatenate([block, from_x, from_y, low, high], axis=0)

    def plane_reduce_even(self, part):
        size = part.shape[0] // 4
        half = size // 2
        own, to_x, to_y, across = (part[i * size : (i + 1) * size] for i in range(4))
        low, high = swap(across[:half], SIDE_X), swap(across[half:], SIDE_Y)
        own, to_x, to_y, low, high = yield (own, to_x, to_y, low, high)
        low = (to_y[:half].astype(f32) + low.astype(f32)).astype(bf16)
        high = (to_x[half:].astype(f32) + high.astype(f32)).astype(bf16)
        to_y = jnp.concatenate([low, to_y[half:]], axis=0)
        to_x = jnp.concatenate([to_x[:half], high], axis=0)
        own, from_x, from_y = yield (own, swap(to_x, SIDE_X), swap(to_y, SIDE_Y))
        return own.astype(f32) + from_x.astype(f32) + from_y.astype(f32)

    def plane_reduce(self, part, slow=0):
        size = part.shape[0] // 4
        rows = part.reshape(2, 2, size, -1)
        arrived = swap(rows[:, 1].reshape(2 * size, -1), SIDE_X)
        yield from pause(slow)
        rows, arrived = yield (rows, arrived)
        rows = rows[:, 0].astype(f32) + arrived.astype(f32).reshape(2, size, -1)
        own, arrived = rows[0], swap(rows[1].astype(bf16), SIDE_Y)
        yield from pause(slow)
        own, arrived = yield (own, arrived)
        return own + arrived.astype(f32)

    def line_gather(self, block, ready):
        ready(0, block)
        rows = [block]
        for r in (1, 2, 3):
            (moved,) = yield (flip(block, r),)
            ready(r, moved)
            rows.append(moved)
        return rows

    def line_reduce(self, parts):
        total = parts[0]
        moved = tuple(flip(parts[r].astype(bf16), r) for r in (1, 2, 3))
        moved = yield moved
        for one in moved:
            total = total + one.astype(f32)
        return total

    def reorder(self, parts):
        place = lax.axis_index("expert")
        odd = (place & 1) == 1
        parts = [jnp.where(odd, parts[i ^ 1], parts[i]) for i in range(4)]
        upper = (place & 2) == 2
        return [jnp.where(upper, parts[i ^ 2], parts[i]) for i in range(4)]

    def order(self):
        return [0, 1, 2, 3]

    def order_back(self):
        return [1, 2, 3, 0]

    def spread(self, blocks, ready, order):
        def plane(r, block, even):
            gather = self.plane_gather_even if even else self.plane_gather
            rows = yield from gather(block)
            ready(r, rows)

        for place, r in enumerate(order):
            if r:
                (moved,) = yield (flip(blocks[r], r),)
                spawn(plane(r, moved, place == 0))
            else:
                spawn(plane(0, blocks[0], place == 0))

    def spread_later(self, blocks, ready):
        def plane(r, block):
            rows = yield from self.plane_gather(block, (SIDE_Y, SIDE_X), slow=1)
            ready(r, rows)

        for r in (1, 2, 3):
            moved = flip(blocks[r], r)
            yield ()
            (moved,) = yield (moved,)
            spawn(plane(r, moved))

    def collect(self, parts, r, part, last=False, slow=0):
        if last:
            mine = yield from self.plane_reduce_even(part)
        else:
            mine = yield from self.plane_reduce(part, slow)
        mine = mine.astype(bf16)
        if r:
            mine = flip(mine, r)
            yield from pause(slow)
            (mine,) = yield (mine,)
        parts[r] = mine
        if len(parts) == self.experts:
            return [parts[i] for i in range(self.experts)]
        return None

    def pair_gather(self, block):
        block, other = yield (block, swap(block, CORE))
        return (block, other)

    def pair_scatter(self, part):
        size = part.shape[0] // 2
        (other,) = yield (swap(part[size:].astype(bf16), CORE),)
        return part[:size].astype(f32) + other.astype(f32)

    def column_gather(self, block):
        moved = tuple(flip(block, r) for r in (1, 2, 3))
        yield ()
        moved = yield moved
        rows = [block] + list(moved)
        mine = jnp.stack(self.reorder(rows))
        mine, other = yield (mine, swap(mine, CORE))
        return (mine, other)

    def column_scatter(self, part):
        (other,) = yield (swap(part[1].astype(bf16), CORE),)
        mine = part[0] + other.astype(f32)
        total = yield from self.line_reduce(self.reorder([mine[i] for i in range(4)]))
        return total

    def steps(self, block, merge):
        for move, masks in ((flip, (1, 2, 3)), (swap, (SIDE_X, SIDE_Y, 6)), (swap, (CORE,))):
            block, *others = yield (block,) + tuple(move(block, mask) for mask in masks)
            for other in others:
                block = merge(block, other)
        return block

    def share(self, index, gains):
        count, size = gains.shape
        piece = jnp.concatenate(
            [index.astype(f32), gains.reshape(1, count * size).astype(f32)]
            + [jnp.zeros((7 - index.shape[0], index.shape[1]), f32)]
        )
        rows = yield from self.steps(piece[None], lambda a, b: jnp.concatenate([a, b]))
        rows = rows.reshape(2, 4, 4, 8, -1)
        index = rows[0].astype(jnp.int32)
        here = lax.axis_index("dp") * 4 + lax.axis_index("expert")
        spots = jnp.arange(32, dtype=jnp.int32)
        core, plane, line = spots // 16, spots // 4 % 4, spots % 4
        relative = plane * 8 + core * 4 + line
        moved = (spots[:, None] ^ here) == relative[None, :]
        gains = rows.reshape(32, 8, -1)[:, 4].astype(bf16)
        gains = jnp.dot(moved.astype(bf16), gains, preferred_element_type=f32)
        gains = gains.reshape(32, count, size).transpose(1, 0, 2).reshape(count, 32 * size)
        return [index[:, r, r] for r in range(4)], gains

    def totals(self, sums, peak):
        width = sums.shape[1]
        peak = jnp.pad(peak[None, :], ((0, 0), (0, width - peak.shape[0])))
        both = jnp.concatenate([sums, peak])
        is_peak = (jnp.arange(both.shape[0]) == sums.shape[0])[:, None]
        both = yield from self.steps(both, lambda a, b: jnp.where(is_peak, jnp.maximum(a, b), a + b))
        place = lax.axis_index("dp") * 4 + lax.axis_index("expert")
        size = width // 32
        mine = lax.dynamic_slice_in_dim(both, place * size, size, 1)
        return mine[:-1], both[-1]


def turn(values, cosine, sine):
    return values * cosine + pltpu.roll(values, HD // 2, 1) * sine


def causal_mask(size):
    keys = lax.broadcasted_iota(jnp.int32, (size, size), 0)
    queries = lax.broadcasted_iota(jnp.int32, (size, size), 1)
    return keys <= queries


def slot_rows(cap, index):
    slots = lax.broadcasted_iota(jnp.int32, (cap, index.shape[1]), 0)
    return (slots == index).astype(f32).astype(bf16)


def assemble_kernel(pair, *refs):
    queries, blocks, out = refs[:pair], refs[pair : 2 * pair], refs[-1]
    count = queries[0].shape[0]
    places, rows = blocks[0].shape[0], blocks[0].shape[1] // 2
    for p in range(pair):
        out[p * count : (p + 1) * count, :] = queries[p][...]
        for z in range(places):
            for kind in range(2):
                first = (kind + 1) * pair * count + p * count + z * rows
                out[first : first + rows, :] = blocks[p][z, kind * rows : (kind + 1) * rows, :]


def assemble(queries, blocks):
    pair = len(queries)
    count, width = queries[0].shape
    places, rows, _ = blocks[0].shape
    part = width // 4
    return pl.pallas_call(
        functools.partial(assemble_kernel, pair),
        grid=(4,),
        in_specs=[pl.BlockSpec((count, part), lambda i: (0, i))] * pair
        + [pl.BlockSpec((places, rows, part), lambda i: (0, 0, i))] * pair,
        out_specs=pl.BlockSpec((3 * pair * count, part), lambda i: (0, i)),
        out_shape=jax.ShapeDtypeStruct((3 * pair * count, width), bf16),
        cost_estimate=pl.CostEstimate(
            flops=0, bytes_accessed=12 * pair * count * width, transcendentals=0
        ),
        compiler_params=pltpu.CompilerParams(vmem_limit_bytes=32 << 20),
        name="assemble",
    )(*queries, *blocks)


def weave_kernel(first_ref, second_ref, out_ref):
    out_ref[:, 0, :] = first_ref[...]
    out_ref[:, 1, :] = second_ref[...]


def weave(first, second):
    count, width = first.shape
    step = 32
    rows = pl.BlockSpec((step, width), lambda i: (i, 0))
    return pl.pallas_call(
        weave_kernel,
        grid=(count // step,),
        in_specs=[rows, rows],
        out_specs=pl.BlockSpec((step, 2, width), lambda i: (i, 0, 0)),
        out_shape=jax.ShapeDtypeStruct((count, 2, width), first.dtype),
        cost_estimate=pl.CostEstimate(
            flops=0, bytes_accessed=16 * count * width, transcendentals=0
        ),
        name="weave",
    )(first, second)


def attend_kernel(
    heads, scale, raw_ref, cos_ref, sin_ref, idx_ref, qkv_ref, mixed_ref, peak_ref
):
    size = cos_ref.shape[0]
    wide = heads * HD
    seqs = raw_ref.shape[0] // size
    cap = mixed_ref.shape[0] // seqs
    cosine, sine = cos_ref[...], sin_ref[...]
    causal = causal_mask(size)
    pairs = [(s, h) for s in range(seqs) for h in range(heads)]
    scores, values = [], []
    for s, h in pairs:
        rows = slice(s * size, (s + 1) * size)
        q_at = slice(h * HD, (h + 1) * HD)
        k_at = slice(wide + h * HD, wide + (h + 1) * HD)
        v_at = slice(2 * wide + h * HD, 2 * wide + (h + 1) * HD)
        query = turn(raw_ref[rows, q_at], cosine, sine).astype(bf16)
        key = turn(raw_ref[rows, k_at], cosine, sine).astype(bf16)
        value = raw_ref[rows, v_at].astype(bf16)
        qkv_ref[rows, q_at] = query
        qkv_ref[rows, k_at] = key
        qkv_ref[rows, v_at] = value
        scores.append(dot_nt(key, query))
        values.append(value)
    scores = [jnp.where(causal, one * scale, masked_value) for one in scores]
    tops = [jnp.max(one, axis=0, keepdims=True) for one in scores]
    shifted = [jnp.exp(one - top) for one, top in zip(scores, tops)]
    totals = [jnp.sum(one, axis=0, keepdims=True) for one in shifted]
    probs = [(one * (1.0 / total)).astype(bf16) for one, total in zip(shifted, totals)]
    mixed = [dot_tn(prob, value).astype(bf16) for prob, value in zip(probs, values)]
    for s in range(seqs):
        index = idx_ref[s]
        for h in range(heads):
            peak_ref[s, h : h + 1, :] = jnp.where(index >= 0, tops[s * heads + h], masked_value)
        joined = jnp.concatenate(mixed[s * heads : (s + 1) * heads], axis=1)
        mixed_ref[s * cap : (s + 1) * cap, :] = dot_nn(slot_rows(cap, index), joined).astype(bf16)


GROUP = 1


def attend(raw, cosine, sine, index, cap):
    seqs, size = index.shape
    wide = raw.shape[1] // 3
    heads = wide // HD
    table = pl.BlockSpec((size, HD), lambda s: (0, 0))
    return pl.pallas_call(
        functools.partial(attend_kernel, heads, HD ** (-0.5)),
        grid=(seqs // GROUP,),
        in_specs=[
            pl.BlockSpec((GROUP * size, 3 * wide), lambda s: (s, 0)),
            table,
            table,
            pl.BlockSpec((GROUP, 1, size), lambda s: (s, 0, 0)),
        ],
        out_specs=[
            pl.BlockSpec((GROUP * size, 3 * wide), lambda s: (s, 0)),
            pl.BlockSpec((GROUP * cap, wide), lambda s: (s, 0)),
            pl.BlockSpec((GROUP, heads, size), lambda s: (s, 0, 0)),
        ],
        out_shape=[
            jax.ShapeDtypeStruct((seqs * size, 3 * wide), bf16),
            jax.ShapeDtypeStruct((seqs * cap, wide), bf16),
            jax.ShapeDtypeStruct((seqs, heads, size), f32),
        ],
        cost_estimate=pl.CostEstimate(
            flops=seqs * heads * size * size * HD * 6,
            bytes_accessed=seqs * size * wide * 20,
            transcendentals=seqs * heads * size * size,
        ),
        compiler_params=pltpu.CompilerParams(vmem_limit_bytes=32 << 20),
        name="attend",
    )(raw, cosine, sine, index[:, None, :])


def attend_back_kernel(heads, scale, qkv_ref, gm_ref, cos_ref, sin_ref, idx_ref, out_ref):
    size = cos_ref.shape[0]
    wide = heads * HD
    seqs = qkv_ref.shape[0] // size
    cap = gm_ref.shape[0] // seqs
    cosine, sine = cos_ref[...], -sin_ref[...]
    causal = causal_mask(size)
    places, operands, scores, grad_probs = [], [], [], []
    for s in range(seqs):
        rows = slice(s * size, (s + 1) * size)
        slots = gm_ref[s * cap : (s + 1) * cap, :]
        grad_mixed = dot_tn(slot_rows(cap, idx_ref[s]), slots).astype(bf16)
        for h in range(heads):
            q_at = slice(h * HD, (h + 1) * HD)
            k_at = slice(wide + h * HD, wide + (h + 1) * HD)
            v_at = slice(2 * wide + h * HD, 2 * wide + (h + 1) * HD)
            query, key, value = qkv_ref[rows, q_at], qkv_ref[rows, k_at], qkv_ref[rows, v_at]
            grad = grad_mixed[:, q_at]
            places.append((rows, q_at, k_at, v_at))
            operands.append((query, key, grad))
            scores.append(dot_nt(key, query))
            grad_probs.append(dot_nt(value, grad))
    scores = [jnp.where(causal, one * scale, masked_value) for one in scores]
    tops = [jnp.max(one, axis=0, keepdims=True) for one in scores]
    shifted = [jnp.exp(one - top) for one, top in zip(scores, tops)]
    totals = [jnp.sum(one, axis=0, keepdims=True) for one in shifted]
    probs = [one * (1.0 / total) for one, total in zip(shifted, totals)]
    inners = [jnp.sum(p * g, axis=0, keepdims=True) for p, g in zip(probs, grad_probs)]
    grads = [(p * (g - i)).astype(bf16) for p, g, i in zip(probs, grad_probs, inners)]
    for place, (query, key, grad), prob, grad_scores in zip(places, operands, probs, grads):
        rows, q_at, k_at, v_at = place
        grad_query = dot_tn(grad_scores, key) * scale
        grad_key = dot_nn(grad_scores, query) * scale
        out_ref[rows, q_at] = turn(grad_query, cosine, sine).astype(bf16)
        out_ref[rows, k_at] = turn(grad_key, cosine, sine).astype(bf16)
        out_ref[rows, v_at] = dot_nn(prob.astype(bf16), grad).astype(bf16)


def attend_back(qkv, grad_mixed, cosine, sine, index):
    seqs, size = index.shape
    cap = grad_mixed.shape[0] // seqs
    wide = qkv.shape[1] // 3
    heads = wide // HD
    table = pl.BlockSpec((size, HD), lambda s: (0, 0))
    return pl.pallas_call(
        functools.partial(attend_back_kernel, heads, HD ** (-0.5)),
        grid=(seqs // GROUP,),
        in_specs=[
            pl.BlockSpec((GROUP * size, 3 * wide), lambda s: (s, 0)),
            pl.BlockSpec((GROUP * cap, wide), lambda s: (s, 0)),
            table,
            table,
            pl.BlockSpec((GROUP, 1, size), lambda s: (s, 0, 0)),
        ],
        out_specs=pl.BlockSpec((GROUP * size, 3 * wide), lambda s: (s, 0)),
        out_shape=jax.ShapeDtypeStruct((seqs * size, 3 * wide), bf16),
        cost_estimate=pl.CostEstimate(
            flops=seqs * heads * size * size * HD * 12,
            bytes_accessed=seqs * size * wide * 14,
            transcendentals=seqs * heads * size * size,
        ),
        compiler_params=pltpu.CompilerParams(vmem_limit_bytes=32 << 20),
        name="attend_back",
    )(qkv, grad_mixed, cosine, sine, index[:, None, :])


def on_device(
    links,
    hidden_in,
    seq_lengths,
    attn_routes,
    attn_gates,
    mlp_routes,
    mlp_gates,
    attn_gain,
    mlp_gain,
    k_weight,
    v_weight,
    attn_experts,
    mlp_experts,
    logit_limit,
    out_grad,
):
    experts = links.experts
    seq_len, width = hidden_in.shape
    cap = seq_len * attn_routes.shape[1] * 3 // (2 * experts)
    shard_heads = attn_experts.shape[1] // HD
    local_heads = shard_heads * links.pair
    wide = local_heads * HD
    dp_id = lax.axis_index("dp")
    places = jnp.arange(seq_len, dtype=jnp.int32)
    live = places < seq_lengths[0]
    labels = links.labels()

    before = (places[:, None] < places[None, :]).astype(bf16)

    def slot_tables(routes, gates):
        first, second = routes[:, 0][None, :], routes[:, 1][None, :]
        names = labels[:, None]
        named = (first == names) | (second == names)
        rank = dot_nn(named.astype(bf16), before).astype(jnp.int32)
        index = jnp.where(named & live[None, :], rank, -1)
        weight = jnp.where(first == names, gates[:, 0][None, :], 0.0) + jnp.where(
            second == names, gates[:, 1][None, :], 0.0
        )
        slot_ids = jnp.arange(cap, dtype=jnp.int32)[None, :, None]
        taken = slot_ids == index[:, None, :]
        combine = jnp.where(taken, weight[:, None, :], 0.0)
        slot_gate = jnp.sum(combine, axis=2)[:, :, None]
        taken = taken.astype(bf16)
        return index, taken, slot_gate, two_parts(combine)

    key_rows = k_weight.shape[0]
    attn_index, attn_taken, attn_slot_gate, attn_combine = slot_tables(attn_routes, attn_gates)
    _, mlp_taken, mlp_slot_gate, mlp_combine = slot_tables(mlp_routes, mlp_gates)
    def combine_rows(parts, rows):
        rows = jnp.concatenate(rows, axis=0)
        flat = [one.reshape(experts * cap, seq_len) for one in parts]
        return sum(dot_tn(one, rows) for one in flat)

    half = HD // 2
    freqs = rope_base ** (-jnp.arange(half, dtype=f32) / half)
    angles = places.astype(f32)[:, None] * freqs[None, :]
    cosine = jnp.concatenate([jnp.cos(angles), jnp.cos(angles)], axis=1)
    sine = jnp.concatenate([-jnp.sin(angles), jnp.sin(angles)], axis=1)

    head_count = logit_limit.shape[0]
    hidden = hidden_in.astype(f32)
    keep = live.astype(f32)[:, None]
    box = {}

    def wait(*names):
        while any(name not in box for name in names):
            yield ()

    def put(name):
        def ready(r, value):
            box[name, r] = value

        return ready

    def gated(values, *names):
        names = [name for name in names if name in box]
        values = yield tuple(values) + tuple(box[name] for name in names)
        for place, name in enumerate(names):
            box[name] = values[len(values) - len(names) + place]
        return values[: len(values) - len(names)]

    def following(order, r):
        place = order.index(r) + 1
        return order[place] if place < len(order) else None

    def hidden_plane(r, block):
        rows = yield from links.plane_gather(block)
        box["hidden", r] = rows

    def fetch_small():
        index, gains = yield from links.share(attn_index, jnp.stack([attn_gain, mlp_gain]))
        gains = gains.astype(f32)
        box["gain_one"], box["gain_two"] = gains[0:1], gains[1:2]
        box["index"] = index

    def fetch_key_value():
        block = jnp.concatenate([k_weight, v_weight], axis=0)
        key_values = yield from links.column_gather(block)
        yield from wait("q_parts")
        box["qkv_w"] = assemble(box["q_parts"], key_values)

    def fetch_hidden():
        spawn(hidden_plane(0, hidden_in))
        for _ in range(links.column_steps):
            yield ()
        yield from links.line_gather(
            hidden_in, lambda r, block: spawn(hidden_plane(r, block)) if r else None
        )
        box["line"] = True

    def fetch_pair(name, block, after=None):
        parts = yield from links.pair_gather(block)
        if after is not None:
            yield from wait(after)
            parts = yield parts
        (box[name],) = yield (jnp.concatenate(parts, axis=0),)

    def fetch_queries():
        box["q_parts"] = yield from links.pair_gather(attn_experts[0, :, 0, :])

    def fetch_grads():
        slots = [
            (mlp_slot_gate[r] * dot_nn(mlp_taken[r], out_grad)).astype(bf16)
            for r in range(experts)
        ]
        if links.pair == 2:
            spawn(grads_plane(slots[0]))
        slots = yield slots
        if links.pair == 1:
            yield from links.spread(slots, put("grad_rows"), links.order())
        else:
            yield from wait("line")
            yield from links.spread_later(slots, put("grad_rows"))

    def grads_plane(block):
        rows = yield from links.plane_gather(block, (SIDE_Y, SIDE_X))
        box["grad_rows", 0] = rows

    def attention():
        parts = {}
        for r in range(experts):
            yield from wait("qkv_w", "o_w", "index", ("hidden", r))
            values = box["hidden", r].astype(f32)
            norm_one = (values * rms_inverse(values) * box["gain_one"]).astype(bf16)
            box["normed", r] = norm_one
            raw = dot_nt(norm_one, box["qkv_w"])
            qkv, mixed, peak = attend(raw, cosine, sine, box["index"][r], cap)
            part = dot_nn(mixed, box["o_w"]).astype(bf16)
            qkv, mixed, peak, part = yield from gated(
                (qkv, mixed, peak, part), ("hidden", r + 1), ("hidden", r + 2)
            )
            box["turned", r], box["mixed", r] = qkv, mixed
            box["started"] = True
            box["peak", r] = peak
            if r == experts - 1:
                box["attended"] = True
            spawn(gather_middle(parts, r, part))

    def gather_middle(parts, r, part):
        rows = yield from links.collect(parts, r, part, r == experts - 1)
        if rows is None:
            return
        middle = hidden + combine_rows(attn_combine, rows)
        norm_two = (middle * rms_inverse(middle) * box["gain_two"]).astype(bf16)
        slots = [dot_nn(mlp_taken[r], norm_two).astype(bf16) for r in range(experts)]
        *slots, box["middle"] = yield slots + [middle]
        spawn(links.spread(slots, put("mlp_rows"), links.order()))

    def unit_grads():
        for r in links.order():
            yield from wait("down_w", ("grad_rows", r))
            later = following(links.order(), r)
            (box["grad_units", r],) = yield from gated(
                (dot_nt(box["grad_rows", r], box["down_w"]),), ("grad_rows", later)
            )

    def feed_forward():
        grad_parts = {}
        for r in links.order():
            yield from wait(("mlp_rows", r), ("grad_units", r))
            rows, grad_units = box["mlp_rows", r], box["grad_units", r]
            gate_pre = dot_nt(rows, box["gate_w"])
            up_pre = dot_nt(rows, box["up_w"])
            gate_sig = jax.nn.sigmoid(gate_pre)
            silu_val = gate_pre * gate_sig
            units = (silu_val * up_pre).astype(bf16)
            grad_gate = grad_units * up_pre * gate_sig * (1.0 + gate_pre * (1.0 - gate_sig))
            grad_gate = grad_gate.astype(bf16)
            grad_up = (grad_units * silu_val).astype(bf16)
            box["units", r], box["grad_gate", r], box["grad_up", r] = units, grad_gate, grad_up
            grad_part = dot_nn(grad_gate, box["gate_w"]) + dot_nn(grad_up, box["up_w"])
            grad_part = grad_part.astype(bf16)
            out_part = dot_nn(units, box["down_w"]).astype(bf16)
            later = following(links.order(), r)
            grad_part, out_part = yield from gated(
                (grad_part, out_part), ("mlp_rows", later), ("grad_units", later)
            )
            spawn(gather_grads(grad_parts, r, grad_part))
            box["out_part", r] = out_part

    def gather_outs():
        parts = {}
        for r in links.order_back():
            (part,) = yield (box["out_part", r],)
            spawn(gather_out(parts, r, part))

    def gather_out(parts, r, part):
        rows = yield from links.collect(parts, r, part)
        if rows is None:
            return
        total = box["middle"] + combine_rows(mlp_combine, rows)
        box["block_out"] = (keep * total).astype(bf16)

    def gather_grads(parts, r, part):
        rows = yield from links.collect(parts, r, part, r == links.order()[-1])
        if rows is None:
            return
        grad_norm_two = combine_rows([mlp_taken], rows)
        grad_mid_norm, box["gain_two_grad"] = norm_back(
            box["middle"], box["gain_two"], grad_norm_two
        )
        grad_middle = out_grad.astype(f32) * keep + grad_mid_norm
        high, low = two_parts(grad_middle)
        slots = [
            (attn_slot_gate[r] * (dot_nn(attn_taken[r], high) + dot_nn(attn_taken[r], low)))
            .astype(bf16)
            for r in range(experts)
        ]
        *slots, box["grad_middle"] = yield slots + [grad_middle]
        spawn(links.spread(slots, put("attn_grad_rows"), links.order_back()))
        spawn(gather_outs())
        spawn(expert_grads())

    def joined(name):
        return jnp.concatenate([box[name, r] for r in range(experts)], axis=0)

    def expert_grads():
        rows, grads = joined("mlp_rows"), joined("grad_rows")
        pieces = []
        for name, other in (("grad_gate", rows), ("grad_up", rows), ("units", grads)):
            (whole,) = yield (dot_tn(joined(name), other).astype(bf16),)
            piece = yield from links.pair_scatter(whole)
            pieces.append(piece)
        box["mlp_grad"] = jnp.stack(pieces).transpose(1, 0, 2)[None]

    def attention_back():
        parts = {}
        *early, last = links.order_back()

        def early_rows(start, stop):
            grads = jnp.concatenate([box["grads", r][:, start:stop] for r in early], axis=0)
            return grads, jnp.concatenate([box["normed", r] for r in early], axis=0)

        for r in links.order_back():
            yield from wait(("attn_grad_rows", r))
            grad_mixed = dot_nt(box["attn_grad_rows", r], box["o_w"]).astype(bf16)
            grads = attend_back(box["turned", r], grad_mixed, cosine, sine, box["index"][r])
            later = following(links.order_back(), r)
            part = dot_nn(grads, box["qkv_w"]).astype(bf16)
            box["grads", r], part = yield from gated((grads, part), ("attn_grad_rows", later))
            spawn(gather_input(parts, r, part))
            if r == early[-1]:
                kv_sum = dot_tn(*early_rows(wide, None))
                q_sum = dot_tn(*early_rows(0, wide))
                kv_sum, q_sum = yield (kv_sum, q_sum)
        grads, rows = box["grads", last], box["normed", last]
        kv_grad = kv_sum + dot_tn(grads[:, wide:], rows)
        gain_one = jnp.sum(kv_grad * box["qkv_w"][wide:].astype(f32), axis=0, keepdims=True)
        kv_grad, grads, rows = yield (kv_grad, grads, rows)
        spawn(project_grads(kv_grad))
        q_grad = q_sum + dot_tn(grads[:, :wide], rows)
        more = jnp.sum(q_grad * box["qkv_w"][:wide].astype(f32), axis=0, keepdims=True)
        (q_grad,) = yield (q_grad,)
        box["gain_one_grad"] = (gain_one + more) / box["gain_one"]
        spawn(gather_totals())
        query_grad = yield from links.pair_scatter(q_grad)
        out_grads = dot_tn(joined("mixed"), joined("attn_grad_rows"))
        (out_grads,) = yield (out_grads,)
        out_grads = yield from links.pair_scatter(out_grads)
        box["attn_grad"] = weave(query_grad, out_grads)[None]

    def gather_totals():
        local_peak = jnp.max(jnp.stack([box["peak", r] for r in range(experts)]), axis=(0, 1, 3))
        owners = jnp.concatenate(
            [(dp_id ^ i) * shard_heads + jnp.arange(shard_heads) for i in range(links.pair)]
        )
        spots = owners[:, None] == jnp.arange(head_count)[None, :]
        peak_vec = jnp.max(jnp.where(spots, local_peak[:, None], masked_value), axis=0)
        gain_sums = jnp.concatenate([box["gain_one_grad"], box["gain_two_grad"][None]])
        box["gains"], box["peaks"] = yield from links.totals(gain_sums, peak_vec)

    def project_grads(part):
        column = (links.pair, experts, key_rows, width)
        part = jnp.concatenate(
            [part[:wide].reshape(column), part[wide:].reshape(column)], axis=2
        )
        total = yield from links.column_scatter(part)
        box["k_grad"], box["v_grad"] = total[:key_rows], total[key_rows:]

    def gather_input(parts, r, part):
        rows = yield from links.collect(parts, r, part, r == links.order_back()[-1])
        if rows is None:
            return
        grad_norm_one = sum(one.astype(f32) for one in rows)
        grad_hid_norm, _ = norm_back(hidden, box["gain_one"], grad_norm_one)
        box["grad_input"] = box["grad_middle"] + grad_hid_norm

    spawn(fetch_key_value())
    spawn(fetch_hidden())
    spawn(fetch_small())
    spawn(fetch_queries())
    spawn(fetch_pair("o_w", attn_experts[0, :, 1, :]))
    spawn(fetch_pair("down_w", mlp_experts[0, :, 2, :], "started"))
    spawn(fetch_pair("gate_w", mlp_experts[0, :, 0, :], "started"))
    spawn(fetch_pair("up_w", mlp_experts[0, :, 1, :], "started"))
    spawn(fetch_grads())
    spawn(attention())
    spawn(unit_grads())
    spawn(feed_forward())
    spawn(attention_back())
    drive()

    factors = logit_limit / jnp.maximum(box["peaks"][:head_count], logit_limit)
    roots = jnp.sqrt(factors)

    def row_scale(first_row, count):
        rows = first_row + jnp.arange(count, dtype=jnp.int32)
        heads = (rows // HD)[:, None] == jnp.arange(head_count)[None, :]
        return jnp.sum(jnp.where(heads, roots[None, :], 0.0), axis=1, keepdims=True)

    query_count = attn_experts.shape[1]
    clipped_query = (
        attn_experts[0, :, 0, :].astype(f32) * row_scale(dp_id * query_count, query_count)
    ).astype(bf16)[None]
    device_id = dp_id * experts + lax.axis_index("expert")
    clipped_key = (
        k_weight.astype(f32) * row_scale(device_id * key_rows, key_rows)
    ).astype(bf16)
    return (
        box["block_out"],
        box["grad_input"],
        box["k_grad"],
        box["v_grad"],
        box["gains"][0],
        box["gains"][1],
        box["attn_grad"],
        box["mlp_grad"],
        clipped_query,
        clipped_key,
        factors,
    )


def solution(mesh):
    paired = mesh.shape["dp"] == 8 and mesh.shape["expert"] == 4
    links = Paired(mesh) if paired else Plain(mesh)
    rows = P(("dp", "expert"), None)
    vec = P(("dp", "expert"))
    weights = P("expert", "dp", None, None)
    return jax.shard_map(
        functools.partial(on_device, links),
        mesh=mesh,
        in_specs=(rows, vec, rows, rows, rows, rows, vec, vec, rows, rows)
        + (weights, weights, P(), rows),
        out_specs=(rows, rows, rows, rows, vec, vec, weights, weights)
        + (P("expert", "dp", None), rows, P()),
        check_vma=False,
    )
```

```python
import functools

import jax
import jax.numpy as jnp
from jax import lax
from jax.experimental import pallas as pl
from jax.experimental.pallas import tpu as pltpu
from jax.sharding import PartitionSpec as P

HD = 128
eps = 1e-06
rope_base = 10000.0
masked_value = -1e30
f32 = jnp.float32
bf16 = jnp.bfloat16


def rms_inverse(values):
    return lax.rsqrt(jnp.mean(values * values, axis=-1, keepdims=True) + eps)


def norm_back(values, gain_vec, grad_out):
    inverse = rms_inverse(values)
    scaled = grad_out * gain_vec
    inner = jnp.mean(scaled * values, axis=-1, keepdims=True)
    grad_values = inverse * scaled - values * inverse * inverse * inverse * inner
    grad_gain = jnp.sum(grad_out * values * inverse, axis=0)
    return (grad_values, grad_gain)


def dot_nt(left, right):
    return lax.dot_general(left, right, (((1,), (1,)), ((), ())), preferred_element_type=f32)


def dot_nn(left, right):
    return lax.dot_general(left, right, (((1,), (0,)), ((), ())), preferred_element_type=f32)


def dot_tn(left, right):
    return lax.dot_general(left, right, (((0,), (0,)), ((), ())), preferred_element_type=f32)


def two_parts(values):
    high = values.astype(bf16)
    return high, (values - high.astype(f32)).astype(bf16)


CORE, SIDE_X, SIDE_Y = 1, 2, 4
flows = []


def spawn(flow):
    flows.append([flow, None])


def pause(steps):
    for _ in range(steps):
        yield ()


def drive():
    while flows:
        due, going = [], []
        for entry in flows:
            try:
                values = entry[0].send(entry[1])
            except StopIteration:
                continue
            going.append((entry, len(values)))
            due.extend(values)
        flows[:] = [entry for entry, _ in going]
        if due:
            due = lax.optimization_barrier(tuple(due))
        place = 0
        for entry, count in going:
            entry[1] = tuple(due[place : place + count])
            place += count


class Plain:
    def __init__(self, mesh):
        self.pair = 1
        self.column_steps = 0
        self.tp = mesh.shape["dp"]
        self.experts = mesh.shape["expert"]

    def labels(self):
        return jnp.arange(self.experts, dtype=jnp.int32)

    def order(self):
        return list(range(self.experts))

    def exchange(self, blocks):
        moved = lax.all_to_all(jnp.stack(blocks), "expert", 0, 0, tiled=True)
        moved = yield tuple(one for one in moved)
        return moved

    def order_back(self):
        return list(range(self.experts))

    def spread(self, blocks, ready, order):
        moved = yield from self.exchange(blocks)
        for r, one in enumerate(moved):
            rows = yield from self.plane_gather(one)
            ready(r, rows)

    def collect(self, parts, r, part, last=False, slow=0):
        parts[r] = yield from self.plane_reduce(part)
        if len(parts) == self.experts:
            moved = yield from self.exchange([parts[i] for i in range(self.experts)])
            return list(moved)
        return None

    def line_gather(self, block, ready):
        rows = lax.all_gather(block, "expert", axis=0, tiled=False)
        rows = yield tuple(one for one in rows)
        for r, one in enumerate(rows):
            ready(r, one)
        return rows

    def plane_gather(self, block, axes=None):
        (rows,) = yield (lax.all_gather(block, "dp", axis=0, tiled=True),)
        return rows

    def plane_reduce(self, part):
        mine = lax.psum_scatter(part.astype(bf16), "dp", scatter_dimension=0, tiled=True)
        (mine,) = yield (mine,)
        return mine

    def share(self, index, gains):
        yield ()
        moved = lax.all_to_all(index[:, None, :], "expert", 0, 0, tiled=True)
        rows = lax.all_gather(moved, "dp", axis=1, tiled=True)
        gains = lax.all_gather(gains, ("dp", "expert"), axis=1, tiled=True)
        return [one for one in rows], gains

    def pair_gather(self, block):
        (block,) = yield (block,)
        return (block,)

    def pair_scatter(self, part):
        (part,) = yield (part,)
        return part.astype(f32)

    def column_gather(self, block):
        (rows,) = yield (lax.all_gather(block, "expert", axis=0, tiled=False),)
        return (rows,)

    def column_scatter(self, part):
        part = part[:, 0].reshape(2, self.experts, -1, part.shape[-1]).astype(bf16)
        total = lax.psum_scatter(part, "expert", scatter_dimension=1, tiled=True)
        (total,) = yield (total,)
        return total.reshape(-1, part.shape[-1]).astype(f32)

    def totals(self, sums, peak):
        yield ()
        sums = lax.psum_scatter(sums, ("dp", "expert"), scatter_dimension=1, tiled=True)
        return sums, lax.pmax(peak, ("dp", "expert"))


def swap(block, mask):
    return lax.ppermute(block, "dp", [(i, i ^ mask) for i in range(8)])


def flip(block, mask):
    return lax.ppermute(block, "expert", [(i, i ^ mask) for i in range(4)])


class Paired:
    def __init__(self, mesh):
        self.pair = 2
        self.column_steps = 2
        self.tp = 4
        self.experts = 4

    def labels(self):
        return lax.axis_index("expert") ^ jnp.arange(4, dtype=jnp.int32)

    def plane_gather(self, block, axes=(SIDE_X, SIDE_Y), slow=0):
        other = swap(block, axes[0])
        yield from pause(slow)
        (other,) = yield (other,)
        both = jnp.concatenate([block, other], axis=0)
        other = swap(both, axes[1])
        yield from pause(slow)
        (other,) = yield (other,)
        if axes[0] == SIDE_X:
            return jnp.concatenate([both, other], axis=0)
        size = block.shape[0]
        return jnp.concatenate([block, other[:size], both[size:], other[size:]], axis=0)

    def plane_gather_even(self, block):
        half = block.shape[0] // 2
        from_x, from_y = yield (swap(block, SIDE_X), swap(block, SIDE_Y))
        low, high = yield (swap(from_y[:half], SIDE_X), swap(from_x[half:], SIDE_Y))
        return jnp.concatenate([block, from_x, from_y, low, high], axis=0)

    def plane_reduce_even(self, part):
        size = part.shape[0] // 4
        half = size // 2
        own, to_x, to_y, across = (part[i * size : (i + 1) * size] for i in range(4))
        low, high = swap(across[:half], SIDE_X), swap(across[half:], SIDE_Y)
        own, to_x, to_y, low, high = yield (own, to_x, to_y, low, high)
        low = (to_y[:half].astype(f32) + low.astype(f32)).astype(bf16)
        high = (to_x[half:].astype(f32) + high.astype(f32)).astype(bf16)
        to_y = jnp.concatenate([low, to_y[half:]], axis=0)
        to_x = jnp.concatenate([to_x[:half], high], axis=0)
        own, from_x, from_y = yield (own, swap(to_x, SIDE_X), swap(to_y, SIDE_Y))
        return own.astype(f32) + from_x.astype(f32) + from_y.astype(f32)

    def plane_reduce(self, part, slow=0):
        size = part.shape[0] // 4
        rows = part.reshape(2, 2, size, -1)
        arrived = swap(rows[:, 1].reshape(2 * size, -1), SIDE_X)
        yield from pause(slow)
        rows, arrived = yield (rows, arrived)
        rows = rows[:, 0].astype(f32) + arrived.astype(f32).reshape(2, size, -1)
        own, arrived = rows[0], swap(rows[1].astype(bf16), SIDE_Y)
        yield from pause(slow)
        own, arrived = yield (own, arrived)
        return own + arrived.astype(f32)

    def line_gather(self, block, ready):
        ready(0, block)
        rows = [block]
        for r in (1, 2, 3):
            (moved,) = yield (flip(block, r),)
            ready(r, moved)
            rows.append(moved)
        return rows

    def line_reduce(self, parts):
        total = parts[0]
        moved = tuple(flip(parts[r].astype(bf16), r) for r in (1, 2, 3))
        moved = yield moved
        for one in moved:
            total = total + one.astype(f32)
        return total

    def reorder(self, parts):
        place = lax.axis_index("expert")
        odd = (place & 1) == 1
        parts = [jnp.where(odd, parts[i ^ 1], parts[i]) for i in range(4)]
        upper = (place & 2) == 2
        return [jnp.where(upper, parts[i ^ 2], parts[i]) for i in range(4)]

    def order(self):
        return [0, 1, 2, 3]

    def order_back(self):
        return [1, 2, 3, 0]

    def spread(self, blocks, ready, order):
        def plane(r, block, even):
            gather = self.plane_gather_even if even else self.plane_gather
            rows = yield from gather(block)
            ready(r, rows)

        for place, r in enumerate(order):
            if r:
                (moved,) = yield (flip(blocks[r], r),)
                spawn(plane(r, moved, place == 0))
            else:
                spawn(plane(0, blocks[0], place == 0))

    def spread_later(self, blocks, ready):
        def plane(r, block):
            rows = yield from self.plane_gather(block, (SIDE_Y, SIDE_X), slow=1)
            ready(r, rows)

        for r in (1, 2, 3):
            moved = flip(blocks[r], r)
            yield ()
            (moved,) = yield (moved,)
            spawn(plane(r, moved))

    def collect(self, parts, r, part, last=False, slow=0):
        if last:
            mine = yield from self.plane_reduce_even(part)
        else:
            mine = yield from self.plane_reduce(part, slow)
        mine = mine.astype(bf16)
        if r:
            mine = flip(mine, r)
            yield from pause(slow)
            (mine,) = yield (mine,)
        parts[r] = mine
        if len(parts) == self.experts:
            return [parts[i] for i in range(self.experts)]
        return None

    def pair_gather(self, block):
        block, other = yield (block, swap(block, CORE))
        return (block, other)

    def pair_scatter(self, part):
        size = part.shape[0] // 2
        (other,) = yield (swap(part[size:].astype(bf16), CORE),)
        return part[:size].astype(f32) + other.astype(f32)

    def column_gather(self, block):
        moved = tuple(flip(block, r) for r in (1, 2, 3))
        yield ()
        moved = yield moved
        rows = [block] + list(moved)
        mine = jnp.stack(self.reorder(rows))
        mine, other = yield (mine, swap(mine, CORE))
        return (mine, other)

    def column_scatter(self, part):
        size, width = part.shape[2] // 4, part.shape[3]
        other = swap(part[:, 1].astype(bf16).reshape(-1, width), CORE)
        own, other = yield (part[:, 0], other)
        mine = own + other.astype(f32).reshape(2, -1, width)
        place = lax.axis_index("expert")
        blocks = [
            lax.dynamic_slice_in_dim(mine, (place ^ r) * size, size, 1).reshape(-1, width)
            for r in range(4)
        ]
        total = yield from self.line_reduce(blocks)
        return total

    def steps(self, block, merge):
        for move, masks in ((flip, (1, 2, 3)), (swap, (SIDE_X, SIDE_Y, 6)), (swap, (CORE,))):
            block, *others = yield (block,) + tuple(move(block, mask) for mask in masks)
            for other in others:
                block = merge(block, other)
        return block

    def share(self, index, gains):
        count, size = gains.shape
        piece = jnp.concatenate(
            [index.astype(f32), gains.reshape(1, count * size).astype(f32)]
            + [jnp.zeros((7 - index.shape[0], index.shape[1]), f32)]
        )
        rows = yield from self.steps(piece[None], lambda a, b: jnp.concatenate([a, b]))
        rows = rows.reshape(2, 4, 4, 8, -1)
        index = rows[0].astype(jnp.int32)
        here = lax.axis_index("dp") * 4 + lax.axis_index("expert")
        spots = jnp.arange(32, dtype=jnp.int32)
        core, plane, line = spots // 16, spots // 4 % 4, spots % 4
        relative = plane * 8 + core * 4 + line
        moved = (spots[:, None] ^ here) == relative[None, :]
        gains = rows.reshape(32, 8, -1)[:, 4].astype(bf16)
        gains = jnp.dot(moved.astype(bf16), gains, preferred_element_type=f32)
        gains = gains.reshape(32, count, size).transpose(1, 0, 2).reshape(count, 32 * size)
        return [index[:, r, r] for r in range(4)], gains

    def totals(self, sums, peak):
        width = sums.shape[1]
        peak = jnp.pad(peak[None, :], ((0, 0), (0, width - peak.shape[0])))
        both = jnp.concatenate([sums, peak])
        is_peak = (jnp.arange(both.shape[0]) == sums.shape[0])[:, None]
        both = yield from self.steps(both, lambda a, b: jnp.where(is_peak, jnp.maximum(a, b), a + b))
        place = lax.axis_index("dp") * 4 + lax.axis_index("expert")
        size = width // 32
        mine = lax.dynamic_slice_in_dim(both, place * size, size, 1)
        return mine[:-1], both[-1]


def turn(values, cosine, sine):
    return values * cosine + pltpu.roll(values, HD // 2, 1) * sine


def causal_mask(size):
    keys = lax.broadcasted_iota(jnp.int32, (size, size), 0)
    queries = lax.broadcasted_iota(jnp.int32, (size, size), 1)
    return keys <= queries


def slot_rows(cap, index):
    slots = lax.broadcasted_iota(jnp.int32, (cap, index.shape[1]), 0)
    return (slots == index).astype(f32).astype(bf16)


def assemble_kernel(pair, *refs):
    queries, blocks, out = refs[:pair], refs[pair : 2 * pair], refs[-1]
    count = queries[0].shape[0]
    places, rows = blocks[0].shape[0], blocks[0].shape[1] // 2
    for p in range(pair):
        out[p * count : (p + 1) * count, :] = queries[p][...]
        for z in range(places):
            for kind in range(2):
                first = (kind + 1) * pair * count + p * count + z * rows
                out[first : first + rows, :] = blocks[p][z, kind * rows : (kind + 1) * rows, :]


def assemble(queries, blocks):
    pair = len(queries)
    count, width = queries[0].shape
    places, rows, _ = blocks[0].shape
    part = width // 4
    return pl.pallas_call(
        functools.partial(assemble_kernel, pair),
        grid=(4,),
        in_specs=[pl.BlockSpec((count, part), lambda i: (0, i))] * pair
        + [pl.BlockSpec((places, rows, part), lambda i: (0, 0, i))] * pair,
        out_specs=pl.BlockSpec((3 * pair * count, part), lambda i: (0, i)),
        out_shape=jax.ShapeDtypeStruct((3 * pair * count, width), bf16),
        cost_estimate=pl.CostEstimate(
            flops=0, bytes_accessed=12 * pair * count * width, transcendentals=0
        ),
        compiler_params=pltpu.CompilerParams(vmem_limit_bytes=32 << 20),
        name="assemble",
    )(*queries, *blocks)


def weave_kernel(first_ref, second_ref, out_ref):
    out_ref[:, 0, :] = first_ref[...]
    out_ref[:, 1, :] = second_ref[...]


def weave(first, second):
    count, width = first.shape
    step = 32
    rows = pl.BlockSpec((step, width), lambda i: (i, 0))
    return pl.pallas_call(
        weave_kernel,
        grid=(count // step,),
        in_specs=[rows, rows],
        out_specs=pl.BlockSpec((step, 2, width), lambda i: (i, 0, 0)),
        out_shape=jax.ShapeDtypeStruct((count, 2, width), first.dtype),
        cost_estimate=pl.CostEstimate(
            flops=0, bytes_accessed=16 * count * width, transcendentals=0
        ),
        name="weave",
    )(first, second)


def attend_kernel(
    heads, scale, raw_ref, cos_ref, sin_ref, idx_ref, qkv_ref, mixed_ref, peak_ref
):
    size = cos_ref.shape[0]
    wide = heads * HD
    seqs = raw_ref.shape[0] // size
    cap = mixed_ref.shape[0] // seqs
    cosine, sine = cos_ref[...], sin_ref[...]
    causal = causal_mask(size)
    pairs = [(s, h) for s in range(seqs) for h in range(heads)]
    scores, values = [], []
    for s, h in pairs:
        rows = slice(s * size, (s + 1) * size)
        q_at = slice(h * HD, (h + 1) * HD)
        k_at = slice(wide + h * HD, wide + (h + 1) * HD)
        v_at = slice(2 * wide + h * HD, 2 * wide + (h + 1) * HD)
        query = turn(raw_ref[rows, q_at], cosine, sine).astype(bf16)
        key = turn(raw_ref[rows, k_at], cosine, sine).astype(bf16)
        value = raw_ref[rows, v_at].astype(bf16)
        qkv_ref[rows, q_at] = query
        qkv_ref[rows, k_at] = key
        qkv_ref[rows, v_at] = value
        scores.append(dot_nt(key, query))
        values.append(value)
    scores = [jnp.where(causal, one * scale, masked_value) for one in scores]
    tops = [jnp.max(one, axis=0, keepdims=True) for one in scores]
    shifted = [jnp.exp(one - top) for one, top in zip(scores, tops)]
    totals = [jnp.sum(one, axis=0, keepdims=True) for one in shifted]
    probs = [(one * (1.0 / total)).astype(bf16) for one, total in zip(shifted, totals)]
    mixed = [dot_tn(prob, value).astype(bf16) for prob, value in zip(probs, values)]
    for s in range(seqs):
        index = idx_ref[s]
        for h in range(heads):
            peak_ref[s, h : h + 1, :] = jnp.where(index >= 0, tops[s * heads + h], masked_value)
        joined = jnp.concatenate(mixed[s * heads : (s + 1) * heads], axis=1)
        mixed_ref[s * cap : (s + 1) * cap, :] = dot_nn(slot_rows(cap, index), joined).astype(bf16)


GROUP = 1


def attend(raw, cosine, sine, index, cap):
    seqs, size = index.shape
    wide = raw.shape[1] // 3
    heads = wide // HD
    table = pl.BlockSpec((size, HD), lambda s: (0, 0))
    return pl.pallas_call(
        functools.partial(attend_kernel, heads, HD ** (-0.5)),
        grid=(seqs // GROUP,),
        in_specs=[
            pl.BlockSpec((GROUP * size, 3 * wide), lambda s: (s, 0)),
            table,
            table,
            pl.BlockSpec((GROUP, 1, size), lambda s: (s, 0, 0)),
        ],
        out_specs=[
            pl.BlockSpec((GROUP * size, 3 * wide), lambda s: (s, 0)),
            pl.BlockSpec((GROUP * cap, wide), lambda s: (s, 0)),
            pl.BlockSpec((GROUP, heads, size), lambda s: (s, 0, 0)),
        ],
        out_shape=[
            jax.ShapeDtypeStruct((seqs * size, 3 * wide), bf16),
            jax.ShapeDtypeStruct((seqs * cap, wide), bf16),
            jax.ShapeDtypeStruct((seqs, heads, size), f32),
        ],
        cost_estimate=pl.CostEstimate(
            flops=seqs * heads * size * size * HD * 6,
            bytes_accessed=seqs * size * wide * 20,
            transcendentals=seqs * heads * size * size,
        ),
        compiler_params=pltpu.CompilerParams(vmem_limit_bytes=32 << 20),
        name="attend",
    )(raw, cosine, sine, index[:, None, :])


def attend_back_kernel(heads, scale, qkv_ref, gm_ref, cos_ref, sin_ref, idx_ref, out_ref):
    size = cos_ref.shape[0]
    wide = heads * HD
    seqs = qkv_ref.shape[0] // size
    cap = gm_ref.shape[0] // seqs
    cosine, sine = cos_ref[...], -sin_ref[...]
    causal = causal_mask(size)
    places, operands, scores, grad_probs = [], [], [], []
    for s in range(seqs):
        rows = slice(s * size, (s + 1) * size)
        slots = gm_ref[s * cap : (s + 1) * cap, :]
        grad_mixed = dot_tn(slot_rows(cap, idx_ref[s]), slots).astype(bf16)
        for h in range(heads):
            q_at = slice(h * HD, (h + 1) * HD)
            k_at = slice(wide + h * HD, wide + (h + 1) * HD)
            v_at = slice(2 * wide + h * HD, 2 * wide + (h + 1) * HD)
            query, key, value = qkv_ref[rows, q_at], qkv_ref[rows, k_at], qkv_ref[rows, v_at]
            grad = grad_mixed[:, q_at]
            places.append((rows, q_at, k_at, v_at))
            operands.append((query, key, grad))
            scores.append(dot_nt(key, query))
            grad_probs.append(dot_nt(value, grad))
    scores = [jnp.where(causal, one * scale, masked_value) for one in scores]
    tops = [jnp.max(one, axis=0, keepdims=True) for one in scores]
    shifted = [jnp.exp(one - top) for one, top in zip(scores, tops)]
    totals = [jnp.sum(one, axis=0, keepdims=True) for one in shifted]
    probs = [one * (1.0 / total) for one, total in zip(shifted, totals)]
    inners = [jnp.sum(p * g, axis=0, keepdims=True) for p, g in zip(probs, grad_probs)]
    grads = [(p * (g - i)).astype(bf16) for p, g, i in zip(probs, grad_probs, inners)]
    for place, (query, key, grad), prob, grad_scores in zip(places, operands, probs, grads):
        rows, q_at, k_at, v_at = place
        grad_query = dot_tn(grad_scores, key) * scale
        grad_key = dot_nn(grad_scores, query) * scale
        out_ref[rows, q_at] = turn(grad_query, cosine, sine).astype(bf16)
        out_ref[rows, k_at] = turn(grad_key, cosine, sine).astype(bf16)
        out_ref[rows, v_at] = dot_nn(prob.astype(bf16), grad).astype(bf16)


def attend_back(qkv, grad_mixed, cosine, sine, index):
    seqs, size = index.shape
    cap = grad_mixed.shape[0] // seqs
    wide = qkv.shape[1] // 3
    heads = wide // HD
    table = pl.BlockSpec((size, HD), lambda s: (0, 0))
    return pl.pallas_call(
        functools.partial(attend_back_kernel, heads, HD ** (-0.5)),
        grid=(seqs // GROUP,),
        in_specs=[
            pl.BlockSpec((GROUP * size, 3 * wide), lambda s: (s, 0)),
            pl.BlockSpec((GROUP * cap, wide), lambda s: (s, 0)),
            table,
            table,
            pl.BlockSpec((GROUP, 1, size), lambda s: (s, 0, 0)),
        ],
        out_specs=pl.BlockSpec((GROUP * size, 3 * wide), lambda s: (s, 0)),
        out_shape=jax.ShapeDtypeStruct((seqs * size, 3 * wide), bf16),
        cost_estimate=pl.CostEstimate(
            flops=seqs * heads * size * size * HD * 12,
            bytes_accessed=seqs * size * wide * 14,
            transcendentals=seqs * heads * size * size,
        ),
        compiler_params=pltpu.CompilerParams(vmem_limit_bytes=32 << 20),
        name="attend_back",
    )(qkv, grad_mixed, cosine, sine, index[:, None, :])


def on_device(
    links,
    hidden_in,
    seq_lengths,
    attn_routes,
    attn_gates,
    mlp_routes,
    mlp_gates,
    attn_gain,
    mlp_gain,
    k_weight,
    v_weight,
    attn_experts,
    mlp_experts,
    logit_limit,
    out_grad,
):
    experts = links.experts
    seq_len, width = hidden_in.shape
    cap = seq_len * attn_routes.shape[1] * 3 // (2 * experts)
    shard_heads = attn_experts.shape[1] // HD
    local_heads = shard_heads * links.pair
    wide = local_heads * HD
    dp_id = lax.axis_index("dp")
    places = jnp.arange(seq_len, dtype=jnp.int32)
    live = places < seq_lengths[0]
    labels = links.labels()

    before = (places[:, None] < places[None, :]).astype(bf16)

    def slot_tables(routes, gates):
        first, second = routes[:, 0][None, :], routes[:, 1][None, :]
        names = labels[:, None]
        named = (first == names) | (second == names)
        rank = dot_nn(named.astype(bf16), before).astype(jnp.int32)
        index = jnp.where(named & live[None, :], rank, -1)
        weight = jnp.where(first == names, gates[:, 0][None, :], 0.0) + jnp.where(
            second == names, gates[:, 1][None, :], 0.0
        )
        slot_ids = jnp.arange(cap, dtype=jnp.int32)[None, :, None]
        taken = slot_ids == index[:, None, :]
        combine = jnp.where(taken, weight[:, None, :], 0.0)
        slot_gate = jnp.sum(combine, axis=2)[:, :, None]
        taken = taken.astype(bf16)
        return index, taken, slot_gate, two_parts(combine)

    key_rows = k_weight.shape[0]
    attn_index, attn_taken, attn_slot_gate, attn_combine = slot_tables(attn_routes, attn_gates)
    _, mlp_taken, mlp_slot_gate, mlp_combine = slot_tables(mlp_routes, mlp_gates)
    def combine_rows(parts, rows):
        rows = jnp.concatenate(rows, axis=0)
        flat = [one.reshape(experts * cap, seq_len) for one in parts]
        return sum(dot_tn(one, rows) for one in flat)

    half = HD // 2
    freqs = rope_base ** (-jnp.arange(half, dtype=f32) / half)
    angles = places.astype(f32)[:, None] * freqs[None, :]
    cosine = jnp.concatenate([jnp.cos(angles), jnp.cos(angles)], axis=1)
    sine = jnp.concatenate([-jnp.sin(angles), jnp.sin(angles)], axis=1)

    head_count = logit_limit.shape[0]
    hidden = hidden_in.astype(f32)
    keep = live.astype(f32)[:, None]
    box = {}

    def wait(*names):
        while any(name not in box for name in names):
            yield ()

    def put(name):
        def ready(r, value):
            box[name, r] = value

        return ready

    def gated(values, *names):
        names = [name for name in names if name in box]
        values = yield tuple(values) + tuple(box[name] for name in names)
        for place, name in enumerate(names):
            box[name] = values[len(values) - len(names) + place]
        return values[: len(values) - len(names)]

    def following(order, r):
        place = order.index(r) + 1
        return order[place] if place < len(order) else None

    def hidden_plane(r, block):
        rows = yield from links.plane_gather(block)
        box["hidden", r] = rows

    def fetch_small():
        index, gains = yield from links.share(attn_index, jnp.stack([attn_gain, mlp_gain]))
        gains = gains.astype(f32)
        box["gain_one"], box["gain_two"] = gains[0:1], gains[1:2]
        box["index"] = index

    def fetch_key_value():
        block = jnp.concatenate([k_weight, v_weight], axis=0)
        key_values = yield from links.column_gather(block)
        yield from wait("q_parts")
        box["qkv_w"] = assemble(box["q_parts"], key_values)

    def fetch_hidden():
        spawn(hidden_plane(0, hidden_in))
        for _ in range(links.column_steps):
            yield ()
        yield from links.line_gather(
            hidden_in, lambda r, block: spawn(hidden_plane(r, block)) if r else None
        )
        box["line"] = True

    def fetch_pair(name, block, after=None):
        parts = yield from links.pair_gather(block)
        if after is not None:
            yield from wait(after)
            parts = yield parts
        (box[name],) = yield (jnp.concatenate(parts, axis=0),)

    def fetch_queries():
        box["q_parts"] = yield from links.pair_gather(attn_experts[0, :, 0, :])

    def fetch_grads():
        slots = [
            (mlp_slot_gate[r] * dot_nn(mlp_taken[r], out_grad)).astype(bf16)
            for r in range(experts)
        ]
        if links.pair == 2:
            spawn(grads_plane(slots[0]))
        slots = yield slots
        if links.pair == 1:
            yield from links.spread(slots, put("grad_rows"), links.order())
        else:
            yield from wait("line")
            yield from links.spread_later(slots, put("grad_rows"))

    def grads_plane(block):
        rows = yield from links.plane_gather(block, (SIDE_Y, SIDE_X))
        box["grad_rows", 0] = rows

    def attention():
        parts = {}
        for r in range(experts):
            yield from wait("qkv_w", "o_w", "index", ("hidden", r))
            values = box["hidden", r].astype(f32)
            norm_one = (values * rms_inverse(values) * box["gain_one"]).astype(bf16)
            box["normed", r] = norm_one
            raw = dot_nt(norm_one, box["qkv_w"])
            qkv, mixed, peak = attend(raw, cosine, sine, box["index"][r], cap)
            part = dot_nn(mixed, box["o_w"]).astype(bf16)
            qkv, mixed, peak, part = yield from gated(
                (qkv, mixed, peak, part), ("hidden", r + 1), ("hidden", r + 2)
            )
            box["turned", r], box["mixed", r] = qkv, mixed
            box["started"] = True
            box["peak", r] = peak
            if r == experts - 1:
                box["attended"] = True
            spawn(gather_middle(parts, r, part))

    def gather_middle(parts, r, part):
        rows = yield from links.collect(parts, r, part, r == experts - 1)
        if rows is None:
            return
        middle = hidden + combine_rows(attn_combine, rows)
        norm_two = (middle * rms_inverse(middle) * box["gain_two"]).astype(bf16)
        slots = [dot_nn(mlp_taken[r], norm_two).astype(bf16) for r in range(experts)]
        *slots, box["middle"] = yield slots + [middle]
        spawn(links.spread(slots, put("mlp_rows"), links.order()))

    def unit_grads():
        for r in links.order():
            yield from wait("down_w", ("grad_rows", r))
            later = following(links.order(), r)
            (box["grad_units", r],) = yield from gated(
                (dot_nt(box["grad_rows", r], box["down_w"]),), ("grad_rows", later)
            )

    def feed_forward():
        grad_parts = {}
        for r in links.order():
            yield from wait(("mlp_rows", r), ("grad_units", r))
            rows, grad_units = box["mlp_rows", r], box["grad_units", r]
            gate_pre = dot_nt(rows, box["gate_w"])
            up_pre = dot_nt(rows, box["up_w"])
            gate_sig = jax.nn.sigmoid(gate_pre)
            silu_val = gate_pre * gate_sig
            units = (silu_val * up_pre).astype(bf16)
            grad_gate = grad_units * up_pre * gate_sig * (1.0 + gate_pre * (1.0 - gate_sig))
            grad_gate = grad_gate.astype(bf16)
            grad_up = (grad_units * silu_val).astype(bf16)
            box["units", r], box["grad_gate", r], box["grad_up", r] = units, grad_gate, grad_up
            grad_part = dot_nn(grad_gate, box["gate_w"]) + dot_nn(grad_up, box["up_w"])
            grad_part = grad_part.astype(bf16)
            out_part = dot_nn(units, box["down_w"]).astype(bf16)
            later = following(links.order(), r)
            grad_part, out_part = yield from gated(
                (grad_part, out_part), ("mlp_rows", later), ("grad_units", later)
            )
            spawn(gather_grads(grad_parts, r, grad_part))
            box["out_part", r] = out_part

    def gather_outs():
        parts = {}
        for r in links.order_back():
            (part,) = yield (box["out_part", r],)
            spawn(gather_out(parts, r, part))

    def gather_out(parts, r, part):
        rows = yield from links.collect(parts, r, part)
        if rows is None:
            return
        total = box["middle"] + combine_rows(mlp_combine, rows)
        box["block_out"] = (keep * total).astype(bf16)

    def gather_grads(parts, r, part):
        rows = yield from links.collect(parts, r, part, r == links.order()[-1])
        if rows is None:
            return
        grad_norm_two = combine_rows([mlp_taken], rows)
        grad_mid_norm, box["gain_two_grad"] = norm_back(
            box["middle"], box["gain_two"], grad_norm_two
        )
        grad_middle = out_grad.astype(f32) * keep + grad_mid_norm
        high, low = two_parts(grad_middle)
        slots = [
            (attn_slot_gate[r] * (dot_nn(attn_taken[r], high) + dot_nn(attn_taken[r], low)))
            .astype(bf16)
            for r in range(experts)
        ]
        *slots, box["grad_middle"] = yield slots + [grad_middle]
        spawn(links.spread(slots, put("attn_grad_rows"), links.order_back()))
        spawn(gather_outs())
        spawn(expert_grads())

    def joined(name):
        return jnp.concatenate([box[name, r] for r in range(experts)], axis=0)

    def expert_grads():
        rows, grads = joined("mlp_rows"), joined("grad_rows")
        pieces = []
        for name, other in (("grad_gate", rows), ("grad_up", rows), ("units", grads)):
            (whole,) = yield (dot_tn(joined(name), other).astype(bf16),)
            piece = yield from links.pair_scatter(whole)
            pieces.append(piece)
        box["mlp_grad"] = jnp.stack(pieces).transpose(1, 0, 2)[None]

    def attention_back():
        parts = {}
        *early, last = links.order_back()

        def early_rows(start, stop):
            grads = jnp.concatenate([box["grads", r][:, start:stop] for r in early], axis=0)
            return grads, jnp.concatenate([box["normed", r] for r in early], axis=0)

        for r in links.order_back():
            yield from wait(("attn_grad_rows", r))
            grad_mixed = dot_nt(box["attn_grad_rows", r], box["o_w"]).astype(bf16)
            grads = attend_back(box["turned", r], grad_mixed, cosine, sine, box["index"][r])
            later = following(links.order_back(), r)
            part = dot_nn(grads, box["qkv_w"]).astype(bf16)
            box["grads", r], part = yield from gated((grads, part), ("attn_grad_rows", later))
            spawn(gather_input(parts, r, part))
        kv_sum, q_sum = (dot_tn(*early_rows(*span)) for span in ((wide, None), (0, wide)))
        grads, rows = box["grads", last], box["normed", last]
        kv_grad = kv_sum + dot_tn(grads[:, wide:], rows)
        kv_grad, grads, rows = yield (kv_grad, grads, rows)
        spawn(project_grads(kv_grad))
        q_grad = q_sum + dot_tn(grads[:, :wide], rows)
        kv_grad, q_grad = yield (kv_grad, q_grad)
        both = jnp.concatenate([q_grad, kv_grad], axis=0)
        gain_one = jnp.sum(both * box["qkv_w"].astype(f32), axis=0, keepdims=True)
        box["gain_one_grad"] = gain_one / box["gain_one"]
        spawn(gather_totals())
        query_grad = yield from links.pair_scatter(q_grad)
        out_grads = dot_tn(joined("mixed"), joined("attn_grad_rows"))
        (out_grads,) = yield (out_grads,)
        out_grads = yield from links.pair_scatter(out_grads)
        box["attn_grad"] = weave(query_grad, out_grads)[None]

    def gather_totals():
        local_peak = jnp.max(jnp.stack([box["peak", r] for r in range(experts)]), axis=(0, 1, 3))
        owners = jnp.concatenate(
            [(dp_id ^ i) * shard_heads + jnp.arange(shard_heads) for i in range(links.pair)]
        )
        spots = owners[:, None] == jnp.arange(head_count)[None, :]
        peak_vec = jnp.max(jnp.where(spots, local_peak[:, None], masked_value), axis=0)
        gain_sums = jnp.concatenate([box["gain_one_grad"], box["gain_two_grad"][None]])
        box["gains"], box["peaks"] = yield from links.totals(gain_sums, peak_vec)

    def project_grads(part):
        total = yield from links.column_scatter(part.reshape(2, links.pair, wide // links.pair, -1))
        box["k_grad"], box["v_grad"] = total[:key_rows], total[key_rows:]

    def gather_input(parts, r, part):
        rows = yield from links.collect(parts, r, part, r == links.order_back()[-1])
        if rows is None:
            return
        grad_norm_one = sum(one.astype(f32) for one in rows)
        grad_hid_norm, _ = norm_back(hidden, box["gain_one"], grad_norm_one)
        box["grad_input"] = box["grad_middle"] + grad_hid_norm

    spawn(fetch_key_value())
    spawn(fetch_hidden())
    spawn(fetch_small())
    spawn(fetch_queries())
    spawn(fetch_pair("o_w", attn_experts[0, :, 1, :]))
    spawn(fetch_pair("down_w", mlp_experts[0, :, 2, :], "started"))
    spawn(fetch_pair("gate_w", mlp_experts[0, :, 0, :], "started"))
    spawn(fetch_pair("up_w", mlp_experts[0, :, 1, :], "started"))
    spawn(fetch_grads())
    spawn(attention())
    spawn(unit_grads())
    spawn(feed_forward())
    spawn(attention_back())
    drive()

    factors = logit_limit / jnp.maximum(box["peaks"][:head_count], logit_limit)
    roots = jnp.sqrt(factors)

    def row_scale(first_row, count):
        rows = first_row + jnp.arange(count, dtype=jnp.int32)
        heads = (rows // HD)[:, None] == jnp.arange(head_count)[None, :]
        return jnp.sum(jnp.where(heads, roots[None, :], 0.0), axis=1, keepdims=True)

    query_count = attn_experts.shape[1]
    clipped_query = (
        attn_experts[0, :, 0, :].astype(f32) * row_scale(dp_id * query_count, query_count)
    ).astype(bf16)[None]
    device_id = dp_id * experts + lax.axis_index("expert")
    clipped_key = (
        k_weight.astype(f32) * row_scale(device_id * key_rows, key_rows)
    ).astype(bf16)
    return (
        box["block_out"],
        box["grad_input"],
        box["k_grad"],
        box["v_grad"],
        box["gains"][0],
        box["gains"][1],
        box["attn_grad"],
        box["mlp_grad"],
        clipped_query,
        clipped_key,
        factors,
    )


def solution(mesh):
    paired = mesh.shape["dp"] == 8 and mesh.shape["expert"] == 4
    links = Paired(mesh) if paired else Plain(mesh)
    rows = P(("dp", "expert"), None)
    vec = P(("dp", "expert"))
    weights = P("expert", "dp", None, None)
    return jax.shard_map(
        functools.partial(on_device, links),
        mesh=mesh,
        in_specs=(rows, vec, rows, rows, rows, rows, vec, vec, rows, rows)
        + (weights, weights, P(), rows),
        out_specs=(rows, rows, rows, rows, vec, vec, weights, weights)
        + (P("expert", "dp", None), rows, P()),
        check_vma=False,
    )
```

```python
import functools

import jax
import jax.numpy as jnp
from jax import lax
from jax.experimental import pallas as pl
from jax.experimental.pallas import tpu as pltpu
from jax.sharding import PartitionSpec as P

HD = 128
eps = 1e-06
rope_base = 10000.0
masked_value = -1e30
f32 = jnp.float32
bf16 = jnp.bfloat16


def rms_inverse(values):
    return lax.rsqrt(jnp.mean(values * values, axis=-1, keepdims=True) + eps)


def norm_back(values, gain_vec, grad_out):
    inverse = rms_inverse(values)
    scaled = grad_out * gain_vec
    inner = jnp.mean(scaled * values, axis=-1, keepdims=True)
    grad_values = inverse * scaled - values * inverse * inverse * inverse * inner
    grad_gain = jnp.sum(grad_out * values * inverse, axis=0)
    return (grad_values, grad_gain)


def dot_nt(left, right):
    return lax.dot_general(left, right, (((1,), (1,)), ((), ())), preferred_element_type=f32)


def dot_nn(left, right):
    return lax.dot_general(left, right, (((1,), (0,)), ((), ())), preferred_element_type=f32)


def dot_tn(left, right):
    return lax.dot_general(left, right, (((0,), (0,)), ((), ())), preferred_element_type=f32)


def two_parts(values):
    high = values.astype(bf16)
    return high, (values - high.astype(f32)).astype(bf16)


CORE, SIDE_X, SIDE_Y = 1, 2, 4
flows = []


def spawn(flow):
    flows.append([flow, None])


def pause(steps):
    for _ in range(steps):
        yield ()


def drive():
    while flows:
        due, going = [], []
        for entry in flows:
            try:
                values = entry[0].send(entry[1])
            except StopIteration:
                continue
            going.append((entry, len(values)))
            due.extend(values)
        flows[:] = [entry for entry, _ in going]
        if due:
            due = lax.optimization_barrier(tuple(due))
        place = 0
        for entry, count in going:
            entry[1] = tuple(due[place : place + count])
            place += count


class Plain:
    def __init__(self, mesh):
        self.pair = 1
        self.column_steps = 0
        self.tp = mesh.shape["dp"]
        self.experts = mesh.shape["expert"]

    def labels(self):
        return jnp.arange(self.experts, dtype=jnp.int32)

    def order(self):
        return list(range(self.experts))

    def exchange(self, blocks):
        moved = lax.all_to_all(jnp.stack(blocks), "expert", 0, 0, tiled=True)
        moved = yield tuple(one for one in moved)
        return moved

    def order_back(self):
        return list(range(self.experts))

    def spread(self, blocks, ready, order):
        moved = yield from self.exchange(blocks)
        for r, one in enumerate(moved):
            rows = yield from self.plane_gather(one)
            ready(r, rows)

    def collect(self, parts, r, part, last=False, slow=0):
        parts[r] = yield from self.plane_reduce(part)
        if len(parts) == self.experts:
            moved = yield from self.exchange([parts[i] for i in range(self.experts)])
            return list(moved)
        return None

    def line_gather(self, block, ready):
        rows = lax.all_gather(block, "expert", axis=0, tiled=False)
        rows = yield tuple(one for one in rows)
        for r, one in enumerate(rows):
            ready(r, one)
        return rows

    def plane_gather(self, block, axes=None):
        (rows,) = yield (lax.all_gather(block, "dp", axis=0, tiled=True),)
        return rows

    def plane_reduce(self, part):
        mine = lax.psum_scatter(part.astype(bf16), "dp", scatter_dimension=0, tiled=True)
        (mine,) = yield (mine,)
        return mine

    def share(self, index, gains):
        yield ()
        moved = lax.all_to_all(index[:, None, :], "expert", 0, 0, tiled=True)
        rows = lax.all_gather(moved, "dp", axis=1, tiled=True)
        gains = lax.all_gather(gains, ("dp", "expert"), axis=1, tiled=True)
        return [one for one in rows], gains

    def pair_gather(self, block):
        (block,) = yield (block,)
        return (block,)

    def pair_scatter(self, part):
        (part,) = yield (part,)
        return part.astype(f32)

    def pair_send(self, part):
        (part,) = yield (part,)
        return (part,)

    def column_gather(self, block):
        (rows,) = yield (lax.all_gather(block, "expert", axis=0, tiled=False),)
        return (rows,)

    def column_scatter(self, part):
        total = lax.psum_scatter(
            part[0].astype(bf16), "expert", scatter_dimension=0, tiled=True
        )
        (total,) = yield (total,)
        return total[0].astype(f32)

    def totals(self, sums, peak):
        yield ()
        sums = lax.psum_scatter(sums, ("dp", "expert"), scatter_dimension=1, tiled=True)
        return sums, lax.pmax(peak, ("dp", "expert"))


def swap(block, mask):
    return lax.ppermute(block, "dp", [(i, i ^ mask) for i in range(8)])


def flip(block, mask):
    return lax.ppermute(block, "expert", [(i, i ^ mask) for i in range(4)])


class Paired:
    def __init__(self, mesh):
        self.pair = 2
        self.column_steps = 2
        self.tp = 4
        self.experts = 4

    def labels(self):
        return lax.axis_index("expert") ^ jnp.arange(4, dtype=jnp.int32)

    def plane_gather(self, block, axes=(SIDE_X, SIDE_Y), slow=0):
        other = swap(block, axes[0])
        yield from pause(slow)
        (other,) = yield (other,)
        both = jnp.concatenate([block, other], axis=0)
        other = swap(both, axes[1])
        yield from pause(slow)
        (other,) = yield (other,)
        if axes[0] == SIDE_X:
            return jnp.concatenate([both, other], axis=0)
        size = block.shape[0]
        return jnp.concatenate([block, other[:size], both[size:], other[size:]], axis=0)

    def plane_gather_even(self, block):
        half = block.shape[0] // 2
        from_x, from_y = yield (swap(block, SIDE_X), swap(block, SIDE_Y))
        low, high = yield (swap(from_y[:half], SIDE_X), swap(from_x[half:], SIDE_Y))
        return jnp.concatenate([block, from_x, from_y, low, high], axis=0)

    def plane_reduce_even(self, part):
        size = part.shape[0] // 4
        half = size // 2
        own, to_x, to_y, across = (part[i * size : (i + 1) * size] for i in range(4))
        low, high = swap(across[:half], SIDE_X), swap(across[half:], SIDE_Y)
        own, to_x, to_y, low, high = yield (own, to_x, to_y, low, high)
        low = (to_y[:half].astype(f32) + low.astype(f32)).astype(bf16)
        high = (to_x[half:].astype(f32) + high.astype(f32)).astype(bf16)
        to_y = jnp.concatenate([low, to_y[half:]], axis=0)
        to_x = jnp.concatenate([to_x[:half], high], axis=0)
        own, from_x, from_y = yield (own, swap(to_x, SIDE_X), swap(to_y, SIDE_Y))
        return own.astype(f32) + from_x.astype(f32) + from_y.astype(f32)

    def plane_reduce(self, part, slow=0):
        size = part.shape[0] // 4
        rows = part.reshape(2, 2, size, -1)
        arrived = swap(rows[:, 1].reshape(2 * size, -1), SIDE_X)
        yield from pause(slow)
        rows, arrived = yield (rows, arrived)
        rows = rows[:, 0].astype(f32) + arrived.astype(f32).reshape(2, size, -1)
        own, arrived = rows[0], swap(rows[1].astype(bf16), SIDE_Y)
        yield from pause(slow)
        own, arrived = yield (own, arrived)
        return own + arrived.astype(f32)

    def line_gather(self, block, ready):
        ready(0, block)
        rows = [block]
        for r in (1, 2, 3):
            (moved,) = yield (flip(block, r),)
            ready(r, moved)
            rows.append(moved)
        return rows

    def line_reduce(self, parts):
        total = parts[0]
        moved = tuple(flip(parts[r].astype(bf16), r) for r in (1, 2, 3))
        moved = yield moved
        for one in moved:
            total = total + one.astype(f32)
        return total

    def reorder(self, parts):
        place = lax.axis_index("expert")
        odd = (place & 1) == 1
        parts = [jnp.where(odd, parts[i ^ 1], parts[i]) for i in range(4)]
        upper = (place & 2) == 2
        return [jnp.where(upper, parts[i ^ 2], parts[i]) for i in range(4)]

    def order(self):
        return [0, 1, 2, 3]

    def order_back(self):
        return [1, 2, 3, 0]

    def spread(self, blocks, ready, order):
        def plane(r, block, even):
            gather = self.plane_gather_even if even else self.plane_gather
            rows = yield from gather(block)
            ready(r, rows)

        for place, r in enumerate(order):
            if r:
                (moved,) = yield (flip(blocks[r], r),)
                spawn(plane(r, moved, place == 0))
            else:
                spawn(plane(0, blocks[0], place == 0))

    def spread_later(self, blocks, ready):
        def plane(r, block):
            rows = yield from self.plane_gather(block, (SIDE_Y, SIDE_X), slow=1)
            ready(r, rows)

        for r in (1, 2, 3):
            moved = flip(blocks[r], r)
            yield ()
            (moved,) = yield (moved,)
            spawn(plane(r, moved))

    def collect(self, parts, r, part, last=False, slow=0):
        if last:
            mine = yield from self.plane_reduce_even(part)
        else:
            mine = yield from self.plane_reduce(part, slow)
        mine = mine.astype(bf16)
        if r:
            mine = flip(mine, r)
            yield from pause(slow)
            (mine,) = yield (mine,)
        parts[r] = mine
        if len(parts) == self.experts:
            return [parts[i] for i in range(self.experts)]
        return None

    def pair_gather(self, block):
        block, other = yield (block, swap(block, CORE))
        return (block, other)

    def pair_send(self, part):
        part, other = yield (part, swap(part[part.shape[0] // 2 :], CORE))
        return (part, other)

    def pair_scatter(self, part):
        size = part.shape[0] // 2
        (other,) = yield (swap(part[size:].astype(bf16), CORE),)
        return part[:size].astype(f32) + other.astype(f32)

    def column_gather(self, block):
        moved = tuple(flip(block, r) for r in (1, 2, 3))
        yield ()
        moved = yield moved
        rows = [block] + list(moved)
        mine = jnp.stack(self.reorder(rows))
        mine, other = yield (mine, swap(mine, CORE))
        return (mine, other)

    def column_scatter(self, part):
        (other,) = yield (swap(part[1].astype(bf16), CORE),)
        mine = part[0] + other.astype(f32)
        total = yield from self.line_reduce(self.reorder([mine[i] for i in range(4)]))
        return total

    def steps(self, block, merge):
        for move, masks in ((flip, (1, 2, 3)), (swap, (SIDE_X, SIDE_Y, 6)), (swap, (CORE,))):
            block, *others = yield (block,) + tuple(move(block, mask) for mask in masks)
            for other in others:
                block = merge(block, other)
        return block

    def share(self, index, gains):
        count, size = gains.shape
        piece = jnp.concatenate(
            [index.astype(f32), gains.reshape(1, count * size).astype(f32)]
            + [jnp.zeros((7 - index.shape[0], index.shape[1]), f32)]
        )
        rows = yield from self.steps(piece[None], lambda a, b: jnp.concatenate([a, b]))
        rows = rows.reshape(2, 4, 4, 8, -1)
        index = rows[0].astype(jnp.int32)
        here = lax.axis_index("dp") * 4 + lax.axis_index("expert")
        spots = jnp.arange(32, dtype=jnp.int32)
        core, plane, line = spots // 16, spots // 4 % 4, spots % 4
        relative = plane * 8 + core * 4 + line
        moved = (spots[:, None] ^ here) == relative[None, :]
        gains = rows.reshape(32, 8, -1)[:, 4].astype(bf16)
        gains = jnp.dot(moved.astype(bf16), gains, preferred_element_type=f32)
        gains = gains.reshape(32, count, size).transpose(1, 0, 2).reshape(count, 32 * size)
        return [index[:, r, r] for r in range(4)], gains

    def totals(self, sums, peak):
        width = sums.shape[1]
        peak = jnp.pad(peak[None, :], ((0, 0), (0, width - peak.shape[0])))
        both = jnp.concatenate([sums, peak])
        is_peak = (jnp.arange(both.shape[0]) == sums.shape[0])[:, None]
        both = yield from self.steps(both, lambda a, b: jnp.where(is_peak, jnp.maximum(a, b), a + b))
        place = lax.axis_index("dp") * 4 + lax.axis_index("expert")
        size = width // 32
        mine = lax.dynamic_slice_in_dim(both, place * size, size, 1)
        return mine[:-1], both[-1]


def turn(values, cosine, sine):
    return values * cosine + pltpu.roll(values, HD // 2, 1) * sine


def causal_mask(size):
    keys = lax.broadcasted_iota(jnp.int32, (size, size), 0)
    queries = lax.broadcasted_iota(jnp.int32, (size, size), 1)
    return keys <= queries


def slot_rows(cap, index):
    slots = lax.broadcasted_iota(jnp.int32, (cap, index.shape[1]), 0)
    return (slots == index).astype(f32).astype(bf16)


def assemble_kernel(pair, *refs):
    queries, blocks, out = refs[:pair], refs[pair : 2 * pair], refs[-1]
    count = queries[0].shape[0]
    places, rows = blocks[0].shape[0], blocks[0].shape[1] // 2
    for p in range(pair):
        out[p * count : (p + 1) * count, :] = queries[p][...]
        for z in range(places):
            for kind in range(2):
                first = (kind + 1) * pair * count + p * count + z * rows
                out[first : first + rows, :] = blocks[p][z, kind * rows : (kind + 1) * rows, :]


def assemble(queries, blocks):
    pair = len(queries)
    count, width = queries[0].shape
    places, rows, _ = blocks[0].shape
    part = width // 4
    return pl.pallas_call(
        functools.partial(assemble_kernel, pair),
        grid=(4,),
        in_specs=[pl.BlockSpec((count, part), lambda i: (0, i))] * pair
        + [pl.BlockSpec((places, rows, part), lambda i: (0, 0, i))] * pair,
        out_specs=pl.BlockSpec((3 * pair * count, part), lambda i: (0, i)),
        out_shape=jax.ShapeDtypeStruct((3 * pair * count, width), bf16),
        cost_estimate=pl.CostEstimate(
            flops=0, bytes_accessed=12 * pair * count * width, transcendentals=0
        ),
        compiler_params=pltpu.CompilerParams(vmem_limit_bytes=32 << 20),
        name="assemble",
    )(*queries, *blocks)


def pair_totals_kernel(pair, *refs):
    out = refs[-1]
    for i in range(out.shape[0]):
        total = refs[i * pair][...].astype(f32)
        for other in refs[i * pair + 1 : (i + 1) * pair]:
            total = total + other[...].astype(f32)
        out[i] = total


def pair_totals(pieces, pair):
    count, width = pieces[0].shape[0] // pair, pieces[0].shape[1]
    step = max(i for i in range(16, 177, 16) if count % i == 0)
    kinds = len(pieces) // pair
    return pl.pallas_call(
        functools.partial(pair_totals_kernel, pair),
        grid=(count // step,),
        in_specs=[pl.BlockSpec((step, width), lambda i: (i, 0))] * len(pieces),
        out_specs=pl.BlockSpec((kinds, step, width), lambda i: (0, i, 0)),
        out_shape=jax.ShapeDtypeStruct((kinds, count, width), f32),
        cost_estimate=pl.CostEstimate(
            flops=kinds * count * width, bytes_accessed=8 * kinds * count * width, transcendentals=0
        ),
        compiler_params=pltpu.CompilerParams(vmem_limit_bytes=40 << 20),
        name="pair_totals",
    )(*pieces)


def weave_kernel(first_ref, second_ref, out_ref):
    out_ref[:, 0, :] = first_ref[...]
    out_ref[:, 1, :] = second_ref[...]


def weave(first, second):
    count, width = first.shape
    step = 32
    rows = pl.BlockSpec((step, width), lambda i: (i, 0))
    return pl.pallas_call(
        weave_kernel,
        grid=(count // step,),
        in_specs=[rows, rows],
        out_specs=pl.BlockSpec((step, 2, width), lambda i: (i, 0, 0)),
        out_shape=jax.ShapeDtypeStruct((count, 2, width), first.dtype),
        cost_estimate=pl.CostEstimate(
            flops=0, bytes_accessed=16 * count * width, transcendentals=0
        ),
        name="weave",
    )(first, second)


def attend_kernel(
    heads, scale, raw_ref, cos_ref, sin_ref, idx_ref, qkv_ref, mixed_ref, peak_ref
):
    size = cos_ref.shape[0]
    wide = heads * HD
    seqs = raw_ref.shape[0] // size
    cap = mixed_ref.shape[0] // seqs
    cosine, sine = cos_ref[...], sin_ref[...]
    causal = causal_mask(size)
    pairs = [(s, h) for s in range(seqs) for h in range(heads)]
    scores, values = [], []
    for s, h in pairs:
        rows = slice(s * size, (s + 1) * size)
        q_at = slice(h * HD, (h + 1) * HD)
        k_at = slice(wide + h * HD, wide + (h + 1) * HD)
        v_at = slice(2 * wide + h * HD, 2 * wide + (h + 1) * HD)
        query = turn(raw_ref[rows, q_at], cosine, sine).astype(bf16)
        key = turn(raw_ref[rows, k_at], cosine, sine).astype(bf16)
        value = raw_ref[rows, v_at].astype(bf16)
        qkv_ref[rows, q_at] = query
        qkv_ref[rows, k_at] = key
        qkv_ref[rows, v_at] = value
        scores.append(dot_nt(key, query))
        values.append(value)
    scores = [jnp.where(causal, one * scale, masked_value) for one in scores]
    tops = [jnp.max(one, axis=0, keepdims=True) for one in scores]
    shifted = [jnp.exp(one - top) for one, top in zip(scores, tops)]
    totals = [jnp.sum(one, axis=0, keepdims=True) for one in shifted]
    probs = [(one * (1.0 / total)).astype(bf16) for one, total in zip(shifted, totals)]
    mixed = [dot_tn(prob, value).astype(bf16) for prob, value in zip(probs, values)]
    for s in range(seqs):
        index = idx_ref[s]
        for h in range(heads):
            peak_ref[s, h : h + 1, :] = jnp.where(index >= 0, tops[s * heads + h], masked_value)
        joined = jnp.concatenate(mixed[s * heads : (s + 1) * heads], axis=1)
        mixed_ref[s * cap : (s + 1) * cap, :] = dot_nn(slot_rows(cap, index), joined).astype(bf16)


GROUP = 1


def attend(raw, cosine, sine, index, cap):
    seqs, size = index.shape
    wide = raw.shape[1] // 3
    heads = wide // HD
    table = pl.BlockSpec((size, HD), lambda s: (0, 0))
    return pl.pallas_call(
        functools.partial(attend_kernel, heads, HD ** (-0.5)),
        grid=(seqs // GROUP,),
        in_specs=[
            pl.BlockSpec((GROUP * size, 3 * wide), lambda s: (s, 0)),
            table,
            table,
            pl.BlockSpec((GROUP, 1, size), lambda s: (s, 0, 0)),
        ],
        out_specs=[
            pl.BlockSpec((GROUP * size, 3 * wide), lambda s: (s, 0)),
            pl.BlockSpec((GROUP * cap, wide), lambda s: (s, 0)),
            pl.BlockSpec((GROUP, heads, size), lambda s: (s, 0, 0)),
        ],
        out_shape=[
            jax.ShapeDtypeStruct((seqs * size, 3 * wide), bf16),
            jax.ShapeDtypeStruct((seqs * cap, wide), bf16),
            jax.ShapeDtypeStruct((seqs, heads, size), f32),
        ],
        cost_estimate=pl.CostEstimate(
            flops=seqs * heads * size * size * HD * 6,
            bytes_accessed=seqs * size * wide * 20,
            transcendentals=seqs * heads * size * size,
        ),
        compiler_params=pltpu.CompilerParams(vmem_limit_bytes=32 << 20),
        name="attend",
    )(raw, cosine, sine, index[:, None, :])


def attend_back_kernel(heads, scale, qkv_ref, gm_ref, cos_ref, sin_ref, idx_ref, out_ref):
    size = cos_ref.shape[0]
    wide = heads * HD
    seqs = qkv_ref.shape[0] // size
    cap = gm_ref.shape[0] // seqs
    cosine, sine = cos_ref[...], -sin_ref[...]
    causal = causal_mask(size)
    places, operands, scores, grad_probs = [], [], [], []
    for s in range(seqs):
        rows = slice(s * size, (s + 1) * size)
        slots = gm_ref[s * cap : (s + 1) * cap, :]
        grad_mixed = dot_tn(slot_rows(cap, idx_ref[s]), slots).astype(bf16)
        for h in range(heads):
            q_at = slice(h * HD, (h + 1) * HD)
            k_at = slice(wide + h * HD, wide + (h + 1) * HD)
            v_at = slice(2 * wide + h * HD, 2 * wide + (h + 1) * HD)
            query, key, value = qkv_ref[rows, q_at], qkv_ref[rows, k_at], qkv_ref[rows, v_at]
            grad = grad_mixed[:, q_at]
            places.append((rows, q_at, k_at, v_at))
            operands.append((query, key, grad))
            scores.append(dot_nt(key, query))
            grad_probs.append(dot_nt(value, grad))
    scores = [jnp.where(causal, one * scale, masked_value) for one in scores]
    tops = [jnp.max(one, axis=0, keepdims=True) for one in scores]
    shifted = [jnp.exp(one - top) for one, top in zip(scores, tops)]
    totals = [jnp.sum(one, axis=0, keepdims=True) for one in shifted]
    probs = [one * (1.0 / total) for one, total in zip(shifted, totals)]
    inners = [jnp.sum(p * g, axis=0, keepdims=True) for p, g in zip(probs, grad_probs)]
    grads = [(p * (g - i)).astype(bf16) for p, g, i in zip(probs, grad_probs, inners)]
    for place, (query, key, grad), prob, grad_scores in zip(places, operands, probs, grads):
        rows, q_at, k_at, v_at = place
        grad_query = dot_tn(grad_scores, key) * scale
        grad_key = dot_nn(grad_scores, query) * scale
        out_ref[rows, q_at] = turn(grad_query, cosine, sine).astype(bf16)
        out_ref[rows, k_at] = turn(grad_key, cosine, sine).astype(bf16)
        out_ref[rows, v_at] = dot_nn(prob.astype(bf16), grad).astype(bf16)


def attend_back(qkv, grad_mixed, cosine, sine, index):
    seqs, size = index.shape
    cap = grad_mixed.shape[0] // seqs
    wide = qkv.shape[1] // 3
    heads = wide // HD
    table = pl.BlockSpec((size, HD), lambda s: (0, 0))
    return pl.pallas_call(
        functools.partial(attend_back_kernel, heads, HD ** (-0.5)),
        grid=(seqs // GROUP,),
        in_specs=[
            pl.BlockSpec((GROUP * size, 3 * wide), lambda s: (s, 0)),
            pl.BlockSpec((GROUP * cap, wide), lambda s: (s, 0)),
            table,
            table,
            pl.BlockSpec((GROUP, 1, size), lambda s: (s, 0, 0)),
        ],
        out_specs=pl.BlockSpec((GROUP * size, 3 * wide), lambda s: (s, 0)),
        out_shape=jax.ShapeDtypeStruct((seqs * size, 3 * wide), bf16),
        cost_estimate=pl.CostEstimate(
            flops=seqs * heads * size * size * HD * 12,
            bytes_accessed=seqs * size * wide * 14,
            transcendentals=seqs * heads * size * size,
        ),
        compiler_params=pltpu.CompilerParams(vmem_limit_bytes=32 << 20),
        name="attend_back",
    )(qkv, grad_mixed, cosine, sine, index[:, None, :])


def on_device(
    links,
    hidden_in,
    seq_lengths,
    attn_routes,
    attn_gates,
    mlp_routes,
    mlp_gates,
    attn_gain,
    mlp_gain,
    k_weight,
    v_weight,
    attn_experts,
    mlp_experts,
    logit_limit,
    out_grad,
):
    experts = links.experts
    seq_len, width = hidden_in.shape
    cap = seq_len * attn_routes.shape[1] * 3 // (2 * experts)
    shard_heads = attn_experts.shape[1] // HD
    local_heads = shard_heads * links.pair
    wide = local_heads * HD
    dp_id = lax.axis_index("dp")
    places = jnp.arange(seq_len, dtype=jnp.int32)
    live = places < seq_lengths[0]
    labels = links.labels()

    before = (places[:, None] < places[None, :]).astype(bf16)

    def slot_tables(routes, gates):
        first, second = routes[:, 0][None, :], routes[:, 1][None, :]
        names = labels[:, None]
        named = (first == names) | (second == names)
        rank = dot_nn(named.astype(bf16), before).astype(jnp.int32)
        index = jnp.where(named & live[None, :], rank, -1)
        weight = jnp.where(first == names, gates[:, 0][None, :], 0.0) + jnp.where(
            second == names, gates[:, 1][None, :], 0.0
        )
        slot_ids = jnp.arange(cap, dtype=jnp.int32)[None, :, None]
        taken = slot_ids == index[:, None, :]
        combine = jnp.where(taken, weight[:, None, :], 0.0)
        slot_gate = jnp.sum(combine, axis=2)[:, :, None]
        taken = taken.astype(bf16)
        return index, taken, slot_gate, two_parts(combine)

    key_rows = k_weight.shape[0]
    attn_index, attn_taken, attn_slot_gate, attn_combine = slot_tables(attn_routes, attn_gates)
    _, mlp_taken, mlp_slot_gate, mlp_combine = slot_tables(mlp_routes, mlp_gates)
    def combine_rows(parts, rows):
        rows = jnp.concatenate(rows, axis=0)
        flat = [one.reshape(experts * cap, seq_len) for one in parts]
        return sum(dot_tn(one, rows) for one in flat)

    half = HD // 2
    freqs = rope_base ** (-jnp.arange(half, dtype=f32) / half)
    angles = places.astype(f32)[:, None] * freqs[None, :]
    cosine = jnp.concatenate([jnp.cos(angles), jnp.cos(angles)], axis=1)
    sine = jnp.concatenate([-jnp.sin(angles), jnp.sin(angles)], axis=1)

    head_count = logit_limit.shape[0]
    hidden = hidden_in.astype(f32)
    keep = live.astype(f32)[:, None]
    box = {}

    def wait(*names):
        while any(name not in box for name in names):
            yield ()

    def put(name):
        def ready(r, value):
            box[name, r] = value

        return ready

    def gated(values, *names):
        names = [name for name in names if name in box]
        values = yield tuple(values) + tuple(box[name] for name in names)
        for place, name in enumerate(names):
            box[name] = values[len(values) - len(names) + place]
        return values[: len(values) - len(names)]

    def following(order, r):
        place = order.index(r) + 1
        return order[place] if place < len(order) else None

    def hidden_plane(r, block):
        rows = yield from links.plane_gather(block)
        box["hidden", r] = rows

    def fetch_small():
        index, gains = yield from links.share(attn_index, jnp.stack([attn_gain, mlp_gain]))
        gains = gains.astype(f32)
        box["gain_one"], box["gain_two"] = gains[0:1], gains[1:2]
        box["index"] = index

    def fetch_key_value():
        block = jnp.concatenate([k_weight, v_weight], axis=0)
        key_values = yield from links.column_gather(block)
        yield from wait("q_parts")
        box["qkv_w"] = assemble(box["q_parts"], key_values)

    def fetch_hidden():
        spawn(hidden_plane(0, hidden_in))
        for _ in range(links.column_steps):
            yield ()
        yield from links.line_gather(
            hidden_in, lambda r, block: spawn(hidden_plane(r, block)) if r else None
        )
        box["line"] = True

    def fetch_pair(name, block, after=None):
        parts = yield from links.pair_gather(block)
        if after is not None:
            yield from wait(after)
            parts = yield parts
        (box[name],) = yield (jnp.concatenate(parts, axis=0),)

    def fetch_queries():
        box["q_parts"] = yield from links.pair_gather(attn_experts[0, :, 0, :])

    def fetch_grads():
        slots = [
            (mlp_slot_gate[r] * dot_nn(mlp_taken[r], out_grad)).astype(bf16)
            for r in range(experts)
        ]
        if links.pair == 2:
            spawn(grads_plane(slots[0]))
        slots = yield slots
        if links.pair == 1:
            yield from links.spread(slots, put("grad_rows"), links.order())
        else:
            yield from wait("line")
            yield from links.spread_later(slots, put("grad_rows"))

    def grads_plane(block):
        rows = yield from links.plane_gather(block, (SIDE_Y, SIDE_X))
        box["grad_rows", 0] = rows

    def attention():
        parts = {}
        for r in range(experts):
            yield from wait("qkv_w", "o_w", "index", ("hidden", r))
            values = box["hidden", r].astype(f32)
            norm_one = (values * rms_inverse(values) * box["gain_one"]).astype(bf16)
            box["normed", r] = norm_one
            raw = dot_nt(norm_one, box["qkv_w"])
            qkv, mixed, peak = attend(raw, cosine, sine, box["index"][r], cap)
            part = dot_nn(mixed, box["o_w"]).astype(bf16)
            qkv, mixed, peak, part = yield from gated(
                (qkv, mixed, peak, part), ("hidden", r + 1), ("hidden", r + 2)
            )
            box["turned", r], box["mixed", r] = qkv, mixed
            box["started"] = True
            box["peak", r] = peak
            if r == experts - 1:
                box["attended"] = True
            spawn(gather_middle(parts, r, part))

    def gather_middle(parts, r, part):
        rows = yield from links.collect(parts, r, part, r == experts - 1)
        if rows is None:
            return
        middle = hidden + combine_rows(attn_combine, rows)
        norm_two = (middle * rms_inverse(middle) * box["gain_two"]).astype(bf16)
        slots = [dot_nn(mlp_taken[r], norm_two).astype(bf16) for r in range(experts)]
        *slots, box["middle"] = yield slots + [middle]
        spawn(links.spread(slots, put("mlp_rows"), links.order()))

    def unit_grads():
        for r in links.order():
            yield from wait("down_w", ("grad_rows", r))
            later = following(links.order(), r)
            (box["grad_units", r],) = yield from gated(
                (dot_nt(box["grad_rows", r], box["down_w"]),), ("grad_rows", later)
            )

    def feed_forward():
        grad_parts = {}
        for r in links.order():
            yield from wait(("mlp_rows", r), ("grad_units", r))
            rows, grad_units = box["mlp_rows", r], box["grad_units", r]
            gate_pre = dot_nt(rows, box["gate_w"])
            up_pre = dot_nt(rows, box["up_w"])
            gate_sig = jax.nn.sigmoid(gate_pre)
            silu_val = gate_pre * gate_sig
            units = (silu_val * up_pre).astype(bf16)
            grad_gate = grad_units * up_pre * gate_sig * (1.0 + gate_pre * (1.0 - gate_sig))
            grad_gate = grad_gate.astype(bf16)
            grad_up = (grad_units * silu_val).astype(bf16)
            box["units", r], box["grad_gate", r], box["grad_up", r] = units, grad_gate, grad_up
            grad_part = dot_nn(grad_gate, box["gate_w"]) + dot_nn(grad_up, box["up_w"])
            grad_part = grad_part.astype(bf16)
            out_part = dot_nn(units, box["down_w"]).astype(bf16)
            later = following(links.order(), r)
            grad_part, out_part = yield from gated(
                (grad_part, out_part), ("mlp_rows", later), ("grad_units", later)
            )
            spawn(gather_grads(grad_parts, r, grad_part))
            box["out_part", r] = out_part

    def gather_outs():
        parts = {}
        for r in links.order_back():
            (part,) = yield (box["out_part", r],)
            spawn(gather_out(parts, r, part))

    def gather_out(parts, r, part):
        rows = yield from links.collect(parts, r, part)
        if rows is None:
            return
        total = box["middle"] + combine_rows(mlp_combine, rows)
        box["block_out"] = (keep * total).astype(bf16)

    def gather_grads(parts, r, part):
        rows = yield from links.collect(parts, r, part, r == links.order()[-1])
        if rows is None:
            return
        grad_norm_two = combine_rows([mlp_taken], rows)
        grad_mid_norm, box["gain_two_grad"] = norm_back(
            box["middle"], box["gain_two"], grad_norm_two
        )
        grad_middle = out_grad.astype(f32) * keep + grad_mid_norm
        high, low = two_parts(grad_middle)
        slots = [
            (attn_slot_gate[r] * (dot_nn(attn_taken[r], high) + dot_nn(attn_taken[r], low)))
            .astype(bf16)
            for r in range(experts)
        ]
        *slots, box["grad_middle"] = yield slots + [grad_middle]
        spawn(links.spread(slots, put("attn_grad_rows"), links.order_back()))
        spawn(gather_outs())
        spawn(expert_grads())

    def joined(name):
        return jnp.concatenate([box[name, r] for r in range(experts)], axis=0)

    def expert_grads():
        rows, grads = joined("mlp_rows"), joined("grad_rows")
        pieces = []
        for name, other in (("grad_gate", rows), ("grad_up", rows), ("units", grads)):
            (whole,) = yield (dot_tn(joined(name), other).astype(bf16),)
            piece = yield from links.pair_send(whole)
            pieces.extend(piece)
        box["mlp_grad"] = pair_totals(pieces, links.pair).transpose(1, 0, 2)[None]

    def attention_back():
        parts = {}
        *early, last = links.order_back()

        def early_rows(start, stop):
            grads = jnp.concatenate([box["grads", r][:, start:stop] for r in early], axis=0)
            return grads, jnp.concatenate([box["normed", r] for r in early], axis=0)

        for r in links.order_back():
            yield from wait(("attn_grad_rows", r))
            grad_mixed = dot_nt(box["attn_grad_rows", r], box["o_w"]).astype(bf16)
            grads = attend_back(box["turned", r], grad_mixed, cosine, sine, box["index"][r])
            later = following(links.order_back(), r)
            part = dot_nn(grads, box["qkv_w"]).astype(bf16)
            box["grads", r], part = yield from gated((grads, part), ("attn_grad_rows", later))
            spawn(gather_input(parts, r, part))
            if r == early[-1]:
                kv_sum = dot_tn(*early_rows(wide, None))
                q_sum = dot_tn(*early_rows(0, wide))
                kv_sum, q_sum = yield (kv_sum, q_sum)
        grads, rows = box["grads", last], box["normed", last]
        kv_grad = kv_sum + dot_tn(grads[:, wide:], rows)
        gain_one = jnp.sum(kv_grad * box["qkv_w"][wide:].astype(f32), axis=0, keepdims=True)
        kv_grad, grads, rows = yield (kv_grad, grads, rows)
        spawn(project_grads(kv_grad))
        q_grad = q_sum + dot_tn(grads[:, :wide], rows)
        more = jnp.sum(q_grad * box["qkv_w"][:wide].astype(f32), axis=0, keepdims=True)
        (q_grad,) = yield (q_grad,)
        box["gain_one_grad"] = (gain_one + more) / box["gain_one"]
        spawn(gather_totals())
        query_grad = yield from links.pair_scatter(q_grad)
        out_grads = dot_tn(joined("mixed"), joined("attn_grad_rows"))
        (out_grads,) = yield (out_grads,)
        out_grads = yield from links.pair_scatter(out_grads)
        box["attn_grad"] = weave(query_grad, out_grads)[None]

    def gather_totals():
        local_peak = jnp.max(jnp.stack([box["peak", r] for r in range(experts)]), axis=(0, 1, 3))
        owners = jnp.concatenate(
            [(dp_id ^ i) * shard_heads + jnp.arange(shard_heads) for i in range(links.pair)]
        )
        spots = owners[:, None] == jnp.arange(head_count)[None, :]
        peak_vec = jnp.max(jnp.where(spots, local_peak[:, None], masked_value), axis=0)
        gain_sums = jnp.concatenate([box["gain_one_grad"], box["gain_two_grad"][None]])
        box["gains"], box["peaks"] = yield from links.totals(gain_sums, peak_vec)

    def project_grads(part):
        column = (links.pair, experts, key_rows, width)
        part = jnp.concatenate(
            [part[:wide].reshape(column), part[wide:].reshape(column)], axis=2
        )
        total = yield from links.column_scatter(part)
        box["k_grad"], box["v_grad"] = total[:key_rows], total[key_rows:]

    def gather_input(parts, r, part):
        rows = yield from links.collect(parts, r, part, r == links.order_back()[-1])
        if rows is None:
            return
        grad_norm_one = sum(one.astype(f32) for one in rows)
        grad_hid_norm, _ = norm_back(hidden, box["gain_one"], grad_norm_one)
        box["grad_input"] = box["grad_middle"] + grad_hid_norm

    spawn(fetch_key_value())
    spawn(fetch_hidden())
    spawn(fetch_small())
    spawn(fetch_queries())
    spawn(fetch_pair("o_w", attn_experts[0, :, 1, :]))
    spawn(fetch_pair("down_w", mlp_experts[0, :, 2, :], "started"))
    spawn(fetch_pair("gate_w", mlp_experts[0, :, 0, :], "started"))
    spawn(fetch_pair("up_w", mlp_experts[0, :, 1, :], "started"))
    spawn(fetch_grads())
    spawn(attention())
    spawn(unit_grads())
    spawn(feed_forward())
    spawn(attention_back())
    drive()

    factors = logit_limit / jnp.maximum(box["peaks"][:head_count], logit_limit)
    roots = jnp.sqrt(factors)

    def row_scale(first_row, count):
        rows = first_row + jnp.arange(count, dtype=jnp.int32)
        heads = (rows // HD)[:, None] == jnp.arange(head_count)[None, :]
        return jnp.sum(jnp.where(heads, roots[None, :], 0.0), axis=1, keepdims=True)

    query_count = attn_experts.shape[1]
    clipped_query = (
        attn_experts[0, :, 0, :].astype(f32) * row_scale(dp_id * query_count, query_count)
    ).astype(bf16)[None]
    device_id = dp_id * experts + lax.axis_index("expert")
    clipped_key = (
        k_weight.astype(f32) * row_scale(device_id * key_rows, key_rows)
    ).astype(bf16)
    return (
        box["block_out"],
        box["grad_input"],
        box["k_grad"],
        box["v_grad"],
        box["gains"][0],
        box["gains"][1],
        box["attn_grad"],
        box["mlp_grad"],
        clipped_query,
        clipped_key,
        factors,
    )


def solution(mesh):
    paired = mesh.shape["dp"] == 8 and mesh.shape["expert"] == 4
    links = Paired(mesh) if paired else Plain(mesh)
    rows = P(("dp", "expert"), None)
    vec = P(("dp", "expert"))
    weights = P("expert", "dp", None, None)
    return jax.shard_map(
        functools.partial(on_device, links),
        mesh=mesh,
        in_specs=(rows, vec, rows, rows, rows, rows, vec, vec, rows, rows)
        + (weights, weights, P(), rows),
        out_specs=(rows, rows, rows, rows, vec, vec, weights, weights)
        + (P("expert", "dp", None), rows, P()),
        check_vma=False,
    )
```
